512 devices in a mesh: dp: 4 (over x), expert: 128 (over y, z, core).
Axes of the slice: x: 4, y: 8, z: 8, core: 2. Of those that a mesh axis runs over, the one named last changes fastest.
Arguments:
- tokens: bfloat16 [24576, 2560], P(('dp', 'expert')), may hold values from -6 to 6
- routes: int32 [4, 24576], P(None, ('dp', 'expert')), may hold values from 0 to 31, as said below
- counts: int32 [512, 128], P(('dp', 'expert')), may hold values from 0 to 2, as said below
- router: bfloat16 [2560, 128], P('dp'), may hold values from -0.125 to 0.125
- gate_up_weight: bfloat16 [128, 768, 2, 2560], P('expert', 'dp'), may hold values from -0.125 to 0.125
- down_weight: bfloat16 [128, 768, 2560], P('expert', 'dp'), may hold values from -0.21875 to 0.21875
- cotangent: bfloat16 [4, 24576, 2560], P(None, ('dp', 'expert')), may hold values from -6 to 6
Outputs:
- routed_out: bfloat16 [4, 24576, 2560], P(None, ('dp', 'expert'))
- token_grad: bfloat16 [24576, 2560], P(('dp', 'expert'))
- router_grad: float32 [2560, 128], P('dp', 'expert')
The draws below stay inside these ranges and needn't reach their ends.
Inputs may be any that keep to these rules, and one draw needn't show every extreme that they name: `routes`: within the 48 tokens of one device, no expert of a member is named by more than 2 of that member's copies; in every draw one expert of each member is named by exactly 2 copies on every device. counts[b, m * 32 + l] is the number of tokens of device b (rows b * 48 to (b + 1) * 48 - 1) whose entry of routes for member m is l.
All inputs are finite; a program needn't handle non-finite values.
Results may differ from the reference program's by a relative error of at most 0.0064.
Values may be sent and summed in bfloat16 or wider, within the bound.
A program may use at most 64 MiB of HBM per device.

```python
import jax
import jax.numpy as jnp
from jax import lax

D = 2560
FFW = 768
MEMBERS = 4
TOK_DEV = 48
EXPERTS = 128
EPM = 32
CAP = 2
TOKENS = 24576
N_DP = 4
N_EXPERT = 128


def route_table(key):
    key = jax.random.fold_in(key, 11)
    key_hot, key_favor, key_noise, key_shuffle = jax.random.split(key, 4)
    blocks = TOKENS // TOK_DEV
    slot_total = EPM * CAP
    slot_expert = jnp.arange(slot_total, dtype=jnp.int32) // CAP
    hot_expert = jax.random.randint(key_hot, (MEMBERS, 1, 1), 0, EPM)
    favor_level = jax.random.randint(key_favor, (MEMBERS, 1, EPM), 0, 4)
    noise_part = jax.random.randint(key_noise, (MEMBERS, blocks, slot_total), 0, 4096)
    scores = jnp.take(favor_level, slot_expert, axis=2) * 1500 + noise_part
    scores = scores + jnp.where(slot_expert[None, None, :] == hot_expert, 65536, 0)
    scores = scores * slot_total + jnp.arange(slot_total, dtype=jnp.int32)[None, None, :]
    _, picked = lax.top_k(scores, TOK_DEV)
    local_ids = picked // CAP
    shuffle_keys = jax.random.randint(key_shuffle, (MEMBERS, blocks, TOK_DEV), 0, 1 << 20) * TOK_DEV + jnp.arange(TOK_DEV, dtype=jnp.int32)[None, None, :]
    shuffle_order = jnp.argsort(shuffle_keys, axis=2)
    local_ids = jnp.take_along_axis(local_ids, shuffle_order, axis=2)
    return local_ids.astype(jnp.int32)


def draw_routes(key, part):
    return route_table(key).reshape(MEMBERS, TOKENS)


def draw_counts(key, part):
    local_ids = route_table(key)
    hit_count = jnp.sum((local_ids[:, :, :, None] == jnp.arange(EPM, dtype=jnp.int32)[None, None, None, :]).astype(jnp.int32), axis=2)
    return jnp.transpose(hit_count, (1, 0, 2)).reshape(TOKENS // TOK_DEV, MEMBERS * EPM)


def levels(rng, dims, cuts, low, high):
    factor_of = 1.0
    for dim, blocks in cuts:
        steps = jax.random.uniform(jax.random.fold_in(jax.random.fold_in(rng, 6), dim), (blocks,), jnp.float32, low / len(cuts), high / len(cuts))
        factor_of = factor_of * jnp.repeat(jnp.exp(steps), dims[dim] // blocks).reshape((-1,) + (1,) * (len(dims) - 1 - dim))
    return factor_of


def gaussian(rng, extent, deviation, reach, pieces=(), held_as=jnp.bfloat16):
    result = deviation * jax.random.normal(rng, extent, jnp.float32)
    if pieces:
        result = result * levels(rng, extent, pieces, -0.22, 0.18)
    return jnp.clip(result, -reach, reach).astype(held_as)


def setup_inputs(seed: int = 0) -> dict:
    seeds = jax.random.split(jax.random.key(seed), 8)
    tokens = gaussian(seeds[0], (TOKENS, D), 1.0, 6.0, ((0, 512),))
    routes = draw_routes(jax.random.fold_in(seeds[7], 71), 0)
    counts = draw_counts(jax.random.fold_in(seeds[7], 71), 0)
    router = gaussian(seeds[3], (D, EXPERTS), D ** -0.5, 0.125, ((0, 4),))
    gate_up_weight = gaussian(seeds[4], (EXPERTS, FFW, 2, D), D ** -0.5, 0.125, ((0, 128), (1, 4)))
    down_weight = gaussian(seeds[5], (EXPERTS, FFW, D), FFW ** -0.5, 0.21875, ((0, 128), (1, 4)))
    cotangent = gaussian(seeds[6], (MEMBERS, TOKENS, D), 1.0, 6.0, ((1, 512),))
    return {"tokens": tokens, "routes": routes, "counts": counts, "router": router, "gate_up_weight": gate_up_weight, "down_weight": down_weight, "cotangent": cotangent}


ROUTE_SCALE = 2.5
BALANCE = 1.0


def expert_pass(tok_rows, grad_rows, gate_weight, up_weight, down_weight):
    contract = (((1,), (1,)), ((), ()))
    gate_pre = lax.dot_general(tok_rows, gate_weight, contract, preferred_element_type=jnp.float32)
    up_pre = lax.dot_general(tok_rows, up_weight, contract, preferred_element_type=jnp.float32)
    squash = jax.nn.sigmoid(gate_pre)
    active = gate_pre * squash
    hidden = (active * up_pre).astype(jnp.bfloat16)
    expert_out = jnp.dot(hidden, down_weight, preferred_element_type=jnp.float32)
    hidden_grad = lax.dot_general(grad_rows, down_weight, contract, preferred_element_type=jnp.float32)
    gate_grad = (hidden_grad * up_pre * squash * (1.0 + gate_pre * (1.0 - squash))).astype(jnp.bfloat16)
    up_grad = (hidden_grad * active).astype(jnp.bfloat16)
    input_grad = jnp.dot(gate_grad, gate_weight, preferred_element_type=jnp.float32) + jnp.dot(up_grad, up_weight, preferred_element_type=jnp.float32)
    return expert_out, input_grad


def reference(tokens, routes, counts, router, gate_up_weight, down_weight, cotangent):
    members, tok_count = routes.shape
    experts = router.shape[1]
    per_member = experts // members
    model_width = tokens.shape[1]
    logits = jnp.dot(tokens, router, preferred_element_type=jnp.float32)
    affinity = jax.nn.sigmoid(logits)
    owners = (routes + per_member * jnp.arange(members, dtype=jnp.int32)[:, None]).astype(jnp.int32)
    gate_values = jnp.take_along_axis(affinity, owners.T, axis=1).T
    out_grad = (ROUTE_SCALE * gate_values[:, :, None] * cotangent.astype(jnp.float32)).astype(jnp.bfloat16)
    copy_count = members * tok_count
    flat_owner = owners.reshape(copy_count)
    copy_tokens = jnp.tile(tokens, (members, 1))
    copy_grads = out_grad.reshape(copy_count, model_width)
    sorted_copies = jnp.argsort(flat_owner, stable=True).astype(jnp.int32)
    expert_sizes = jnp.sum((flat_owner[:, None] == jnp.arange(experts, dtype=jnp.int32)[None, :]).astype(jnp.int32), axis=0)
    starts = (jnp.cumsum(expert_sizes) - expert_sizes).astype(jnp.int32)
    most_rows = N_DP * N_EXPERT * CAP
    lane_index = jnp.arange(most_rows, dtype=jnp.int32)

    def one_expert(buffers, expert_id):
        out_buffer, grad_buffer = buffers
        is_live = lane_index < expert_sizes[expert_id]
        position = jnp.minimum(starts[expert_id] + lane_index, copy_count - 1).astype(jnp.int32)
        picked = sorted_copies[position]
        target = jnp.where(is_live, picked, copy_count).astype(jnp.int32)
        tok_rows = jnp.where(is_live[:, None], copy_tokens[picked], jnp.zeros((), jnp.bfloat16))
        grad_rows = jnp.where(is_live[:, None], copy_grads[picked], jnp.zeros((), jnp.bfloat16))
        pair_weight = gate_up_weight[expert_id]
        expert_out, input_grad = expert_pass(tok_rows, grad_rows, pair_weight[:, 0, :], pair_weight[:, 1, :], down_weight[expert_id])
        out_buffer = out_buffer.at[target].set(expert_out.astype(jnp.bfloat16), mode="drop")
        grad_buffer = grad_buffer.at[target].set(input_grad.astype(jnp.bfloat16), mode="drop")
        return (out_buffer, grad_buffer), None

    blank = jnp.zeros((copy_count, model_width), jnp.bfloat16)
    (copy_out, copy_back), _ = lax.scan(one_expert, (blank, blank), jnp.arange(experts, dtype=jnp.int32))
    expert_out = copy_out.reshape(members, tok_count, model_width)
    routed_out = (ROUTE_SCALE * gate_values[:, :, None] * expert_out.astype(jnp.float32)).astype(jnp.bfloat16)
    affinity_grad = ROUTE_SCALE * jnp.sum(cotangent.astype(jnp.float32) * expert_out.astype(jnp.float32), axis=2)
    expert_load = jnp.sum(counts, axis=0)
    balance = per_member * expert_load.astype(jnp.float32) / tok_count
    chosen = (owners[:, :, None] == jnp.arange(experts, dtype=jnp.int32)[None, None, :]).astype(jnp.float32)
    routed_grad = jnp.sum(chosen * affinity_grad[:, :, None], axis=0)
    logit_grad = (affinity * (1.0 - affinity) * (BALANCE * balance[None, :] + routed_grad)).astype(jnp.bfloat16)
    back_sum = jnp.sum(copy_back.reshape(members, tok_count, model_width).astype(jnp.float32), axis=0)
    router_back = lax.dot_general(logit_grad, router, (((1,), (1,)), ((), ())), preferred_element_type=jnp.float32)
    token_grad = (back_sum + router_back).astype(jnp.bfloat16)
    router_grad = lax.dot_general(tokens, logit_grad, (((0,), (0,)), ((), ())), preferred_element_type=jnp.float32) * (tok_count ** -0.5)
    return routed_out, token_grad, router_grad
```

```python
import functools

import jax
import jax.numpy as jnp
from jax import lax
from jax.experimental import pallas as pl
from jax.experimental.pallas import tpu as pltpu
from jax.sharding import PartitionSpec as P

ROUTE_SCALE = 2.5
BALANCE = 1.0
CAP = 2
STRIDE = 37
MESH = pl.DeviceIdType.MESH
BF16 = jnp.bfloat16
F32 = jnp.float32


def remote(src, dst, send_sem, recv_sem, device):
    return pltpu.make_async_remote_copy(
        src_ref=src,
        dst_ref=dst,
        send_sem=send_sem,
        recv_sem=recv_sem,
        device_id=device,
        device_id_type=MESH,
    )


def take_all(ref, count, sem):
    block = ref.at[pl.ds(0, count)]
    pltpu.make_async_copy(block, block, sem).wait()


def send_kernel(
    n_dp,
    n_exp,
    rows_ref,
    terms_ref,
    pair_ref,
    down_ref,
    rows_out,
    terms_out,
    pair_out,
    down_out,
    row_sems,
    term_sems,
    self_sems,
    own_send,
    own_recv,
    pass_send,
    pass_recv,
):
    d = lax.axis_index("dp")
    e = lax.axis_index("expert")
    sides = ((d + 1) % n_dp, (d + n_dp - 1) % n_dp)
    pair_step = pair_ref.shape[0] // 4
    down_step = down_ref.shape[0] // 2

    def piece(refs, shard, chunk):
        if chunk < 4:
            ref, part = refs[0], pl.ds(chunk * pair_step, pair_step)
        else:
            ref, part = refs[1], pl.ds((chunk - 4) * down_step, down_step)
        return ref.at[part] if shard is None else ref.at[shard, part]

    held = (pair_ref, down_ref)
    full = (pair_out, down_out)
    orders = ((0, 1, 2, 3, 4, 5), (3, 4, 5, 0, 1, 2))

    def own(side, chunk):
        return remote(
            piece(held, None, chunk),
            piece(full, d, chunk),
            own_send.at[side, chunk],
            own_recv.at[side, chunk],
            (sides[side], e),
        )

    def passed(side, chunk):
        source = sides[1 - side]
        return remote(
            piece(full, source, chunk),
            piece(full, source, chunk),
            pass_send.at[side, chunk % 3],
            pass_recv.at[side, chunk % 3],
            (sides[side], e),
        )

    for step in range(6):
        for side in range(2):
            own(side, orders[side][step]).start()
    locals_ = (
        pltpu.make_async_copy(pair_ref, pair_out.at[d], self_sems.at[0]),
        pltpu.make_async_copy(down_ref, down_out.at[d], self_sems.at[1]),
        pltpu.make_async_copy(rows_ref.at[e], rows_out.at[e], self_sems.at[2]),
        pltpu.make_async_copy(terms_ref.at[e], terms_out.at[e], self_sems.at[3]),
    )
    for copy in locals_:
        copy.start()

    def to_peer(s, carry):
        peer = (e + (s * STRIDE) % n_exp) % n_exp
        remote(
            rows_ref.at[peer], rows_out.at[e], row_sems.at[0], row_sems.at[1], (d, peer)
        ).start()
        remote(
            terms_ref.at[peer], terms_out.at[e], term_sems.at[0], term_sems.at[1], (d, peer)
        ).start()
        return carry

    lax.fori_loop(1, n_exp, to_peer, 0)

    for step in range(3):
        for side in range(2):
            chunk = orders[side][step]
            own(side, chunk).wait_recv()
            passed(side, chunk).start()
    for step in range(3, 6):
        for side in range(2):
            own(side, orders[side][step]).wait_recv()
    for copy in locals_:
        copy.wait()
    for step in range(6):
        for side in range(2):
            own(side, orders[side][step]).wait_send()
    for step in range(3):
        for side in range(2):
            passed(side, orders[side][step]).wait()
    take_all(rows_ref, n_exp - 1, row_sems.at[0])
    take_all(rows_out, n_exp - 1, row_sems.at[1])
    take_all(terms_ref, n_exp - 1, term_sems.at[0])
    take_all(terms_out, n_exp - 1, term_sems.at[1])


def return_kernel(
    n_dp, n_exp, rows_ref, sums_ref, rows_out, sums_out, row_sems, self_sems, sum_sems
):
    d = lax.axis_index("dp")
    e = lax.axis_index("expert")

    def small(step):
        peer = (d + step) % n_dp
        return remote(
            sums_ref.at[peer], sums_out.at[d], sum_sems.at[0, step], sum_sems.at[1, step], (peer, e)
        )

    for step in range(1, n_dp):
        small(step).start()
    locals_ = (
        pltpu.make_async_copy(rows_ref.at[e], rows_out.at[e], self_sems.at[0]),
        pltpu.make_async_copy(sums_ref.at[d], sums_out.at[d], self_sems.at[1]),
    )
    for copy in locals_:
        copy.start()

    def to_peer(s, carry):
        peer = (e + (s * STRIDE) % n_exp) % n_exp
        remote(
            rows_ref.at[peer], rows_out.at[e], row_sems.at[0], row_sems.at[1], (d, peer)
        ).start()
        return carry

    lax.fori_loop(1, n_exp, to_peer, 0)
    for copy in locals_:
        copy.wait()
    for step in range(1, n_dp):
        small(step).wait()
    take_all(rows_ref, n_exp - 1, row_sems.at[0])
    take_all(rows_out, n_exp - 1, row_sems.at[1])


def send_all(n_dp, n_exp, rows, terms, pair, down):
    def like(array):
        return jax.ShapeDtypeStruct(array.shape, array.dtype)

    def gathered(array):
        return jax.ShapeDtypeStruct((n_dp, *array.shape), array.dtype)

    dma = pltpu.SemaphoreType.DMA
    return pl.pallas_call(
        functools.partial(send_kernel, n_dp, n_exp),
        name="send_all",
        out_shape=(like(rows), like(terms), gathered(pair), gathered(down)),
        in_specs=[pl.BlockSpec(memory_space=pl.ANY)] * 4,
        out_specs=[pl.BlockSpec(memory_space=pl.ANY)] * 4,
        scratch_shapes=[
            dma((2,)),
            dma((2,)),
            dma((4,)),
            dma((2, 6)),
            dma((2, 6)),
            dma((2, 3)),
            dma((2, 3)),
        ],
        compiler_params=pltpu.CompilerParams(has_side_effects=True),
    )(rows, terms, pair, down)


def return_all(n_dp, n_exp, rows, sums):
    def like(array):
        return jax.ShapeDtypeStruct(array.shape, array.dtype)

    dma = pltpu.SemaphoreType.DMA
    return pl.pallas_call(
        functools.partial(return_kernel, n_dp, n_exp),
        name="return_all",
        out_shape=(like(rows), like(sums)),
        in_specs=[pl.BlockSpec(memory_space=pl.ANY)] * 2,
        out_specs=[pl.BlockSpec(memory_space=pl.ANY)] * 2,
        scratch_shapes=[dma((2,)), dma((2,)), dma((2, n_dp))],
        compiler_params=pltpu.CompilerParams(has_side_effects=True),
    )(rows, sums)


def expert_pass(tok_rows, grad_rows, gate_weight, up_weight, down_weight):
    contract = (((1,), (1,)), ((), ()))
    gate_pre = lax.dot_general(tok_rows, gate_weight, contract, preferred_element_type=F32)
    up_pre = lax.dot_general(tok_rows, up_weight, contract, preferred_element_type=F32)
    squash = jax.nn.sigmoid(gate_pre)
    active = gate_pre * squash
    hidden = (active * up_pre).astype(BF16)
    expert_out = jnp.dot(hidden, down_weight, preferred_element_type=F32)
    hidden_grad = lax.dot_general(grad_rows, down_weight, contract, preferred_element_type=F32)
    gate_grad = (hidden_grad * up_pre * squash * (1.0 + gate_pre * (1.0 - squash))).astype(BF16)
    up_grad = (hidden_grad * active).astype(BF16)
    input_grad = jnp.dot(gate_grad, gate_weight, preferred_element_type=F32) + jnp.dot(
        up_grad, up_weight, preferred_element_type=F32
    )
    return (expert_out, input_grad)


def on_device(n_dp, n_exp, tokens, routes, counts, router, gate_up_weight, down_weight, cotangent):
    members, tok_local = routes.shape
    width = tokens.shape[1]
    experts = router.shape[1]
    per_member = experts // members
    copies = members * tok_local
    tok_total = tok_local * n_dp * n_exp
    half = width // 2
    part = width // n_dp
    slots = experts * CAP
    mine = lax.axis_index("expert")

    router_full = lax.all_gather(router, "dp", axis=0, tiled=True)
    logits = jnp.dot(tokens, router_full, preferred_element_type=F32)
    affinity = jax.nn.sigmoid(logits)
    slope = affinity * (1.0 - affinity)
    dense = lax.dot_general(
        slope.astype(BF16), tokens, (((0,), (0,)), ((), ())), preferred_element_type=F32
    ).astype(BF16)
    spare = jnp.zeros((experts, experts), BF16)
    held = jnp.broadcast_to(counts.astype(BF16), (experts, experts))
    terms = jnp.concatenate([dense[:, :half], held, dense[:, half:], spare], axis=1)
    terms = terms.reshape(experts, 2, half + experts)

    earlier = (
        (routes[:, :, None] == routes[:, None, :])
        & (jnp.arange(tok_local)[None, None, :] < jnp.arange(tok_local)[None, :, None])
    ).astype(jnp.int32)
    rank = jnp.sum(earlier, axis=2)
    owners = routes + per_member * jnp.arange(members, dtype=jnp.int32)[:, None]
    first = owners * (2 * CAP) + rank
    row_ids = jnp.arange(2 * slots, dtype=jnp.int32)
    token_hits = jnp.any(row_ids[:, None, None] == first[None, :, :], axis=1)
    copy_hits = row_ids[:, None] == (first + CAP).reshape(1, copies)
    placing = jnp.concatenate([token_hits, copy_hits], axis=1).astype(BF16)
    stacked = jnp.concatenate([tokens, cotangent.reshape(copies, width)], axis=0)
    rows = (
        jnp.dot(placing, stacked, preferred_element_type=F32)
        .astype(BF16)
        .reshape(experts, 2 * CAP, width)
    )

    rows_in, terms_in, pair_full, down_full = send_all(
        n_dp, n_exp, rows, terms, gate_up_weight[0], down_weight[0]
    )

    tok_rows = rows_in[:, :CAP, :].reshape(slots, width)
    cot_rows = rows_in[:, CAP:, :].reshape(slots, width).astype(F32)
    row_logits = jnp.dot(tok_rows, router_full, preferred_element_type=F32)
    is_mine = (jnp.arange(experts, dtype=jnp.int32) == mine).astype(F32)
    gate = jax.nn.sigmoid(jnp.sum(row_logits * is_mine[None, :], axis=1, keepdims=True))
    router_column = jnp.sum(router_full.astype(F32) * is_mine[None, :], axis=1)
    grad_rows = (ROUTE_SCALE * gate * cot_rows).astype(BF16)
    pair = pair_full.reshape(-1, 2, width)
    expert_out, input_grad = expert_pass(
        tok_rows, grad_rows, pair[:, 0, :], pair[:, 1, :], down_full.reshape(-1, width)
    )
    expert_out = expert_out.astype(BF16).astype(F32)
    routed_rows = (ROUTE_SCALE * gate * expert_out).astype(BF16)
    affinity_grad = ROUTE_SCALE * jnp.sum(cot_rows * expert_out, axis=1, keepdims=True)
    lift = gate * (1.0 - gate) * affinity_grad
    back_rows = (input_grad + lift * router_column[None, :]).astype(BF16)
    routed_sum = lax.dot_general(
        lift.astype(BF16), tok_rows, (((0,), (0,)), ((), ())), preferred_element_type=F32
    )
    terms_sum = jnp.sum(terms_in.astype(F32), axis=0)
    dense_sum = terms_sum[:, :half].reshape(n_dp, part)
    load = jnp.broadcast_to(terms_sum[:1, half:], (n_dp, experts))
    sums = jnp.concatenate([dense_sum, routed_sum.reshape(n_dp, part), load], axis=1)
    short = -sums.shape[1] % 1024
    sums = jnp.pad(sums, ((0, 0), (0, short))).reshape(n_dp, 8, -1)
    results = jnp.concatenate(
        [back_rows.reshape(experts, CAP, width), routed_rows.reshape(experts, CAP, width)], axis=1
    )

    results_in, sums_in = return_all(n_dp, n_exp, results, sums)

    home = lax.dot_general(
        placing,
        results_in.reshape(2 * slots, width),
        (((0,), (0,)), ((), ())),
        preferred_element_type=F32,
    )
    total = jnp.sum(sums_in, axis=0).reshape(-1)
    balance = per_member * total[2 * part : 2 * part + experts] / tok_total
    router_grad = (
        BALANCE * jnp.sum(balance * is_mine) * total[:part] + total[part : 2 * part]
    ) * tok_total ** (-0.5)
    spread = (slope * (BALANCE * balance)[None, :]).astype(BF16)
    router_back = lax.dot_general(
        spread, router_full, (((1,), (1,)), ((), ())), preferred_element_type=F32
    )
    token_grad = (home[:tok_local] + router_back).astype(BF16)
    routed_out = home[tok_local:].astype(BF16).reshape(members, tok_local, width)
    return (routed_out, token_grad, router_grad[:, None])


def solution(mesh):
    in_specs = (
        P(("dp", "expert"), None),
        P(None, ("dp", "expert")),
        P(("dp", "expert"), None),
        P("dp", None),
        P("expert", "dp", None, None),
        P("expert", "dp", None),
        P(None, ("dp", "expert"), None),
    )
    out_specs = (P(None, ("dp", "expert"), None), P(("dp", "expert"), None), P("dp", "expert"))
    sizes = (mesh.shape["dp"], mesh.shape["expert"])
    return jax.shard_map(
        functools.partial(on_device, *sizes),
        mesh=mesh,
        in_specs=in_specs,
        out_specs=out_specs,
        check_vma=False,
    )
```

```python
import functools

import jax
import jax.numpy as jnp
import numpy as np
from jax import lax
from jax.experimental import pallas as pl
from jax.experimental.pallas import tpu as pltpu
from jax.sharding import PartitionSpec as P

ROUTE_SCALE = 2.5
BALANCE = 1.0
CAP = 2
STRIDE = 37
MESH = pl.DeviceIdType.MESH
BF16 = jnp.bfloat16
F32 = jnp.float32


def remote(src, dst, send_sem, recv_sem, device):
    return pltpu.make_async_remote_copy(
        src_ref=src,
        dst_ref=dst,
        send_sem=send_sem,
        recv_sem=recv_sem,
        device_id=device,
        device_id_type=MESH,
    )


def take_all(ref, count, sem):
    block = ref.at[pl.ds(0, count)]
    pltpu.make_async_copy(block, block, sem).wait()


def send_kernel(
    n_dp,
    n_exp,
    rows_ref,
    terms_ref,
    gate_ref,
    up_ref,
    down_ref,
    rows_out,
    terms_out,
    gate_out,
    up_out,
    down_out,
    row_sems,
    term_sems,
    self_sems,
    own_send,
    own_recv,
    pass_send,
    pass_recv,
):
    d = lax.axis_index("dp")
    e = lax.axis_index("expert")
    sides = ((d + 1) % n_dp, (d + n_dp - 1) % n_dp)
    span = gate_ref.shape[0] // 2
    held = (gate_ref, up_ref, down_ref)
    full = (gate_out, up_out, down_out)

    def piece(refs, shard, chunk):
        ref, part = refs[chunk // 2], pl.ds(chunk % 2 * span, span)
        return ref.at[part] if shard is None else ref.at[shard, part]

    orders = ((0, 1, 2, 3, 4, 5), (3, 4, 5, 0, 1, 2))

    def own(side, chunk):
        return remote(
            piece(held, None, chunk),
            piece(full, d, chunk),
            own_send.at[side, chunk],
            own_recv.at[side, chunk],
            (sides[side], e),
        )

    def passed(side, chunk):
        source = sides[1 - side]
        return remote(
            piece(full, source, chunk),
            piece(full, source, chunk),
            pass_send.at[side, chunk % 3],
            pass_recv.at[side, chunk % 3],
            (sides[side], e),
        )

    for step in range(6):
        for side in range(2):
            own(side, orders[side][step]).start()
    locals_ = (
        pltpu.make_async_copy(gate_ref, gate_out.at[d], self_sems.at[0]),
        pltpu.make_async_copy(up_ref, up_out.at[d], self_sems.at[1]),
        pltpu.make_async_copy(down_ref, down_out.at[d], self_sems.at[4]),
        pltpu.make_async_copy(rows_ref.at[e], rows_out.at[e], self_sems.at[2]),
        pltpu.make_async_copy(terms_ref.at[e], terms_out.at[e], self_sems.at[3]),
    )
    for copy in locals_:
        copy.start()

    def to_peer(s, carry):
        peer = (e + (s * STRIDE) % n_exp) % n_exp
        remote(
            rows_ref.at[peer], rows_out.at[e], row_sems.at[0], row_sems.at[1], (d, peer)
        ).start()
        remote(
            terms_ref.at[peer], terms_out.at[e], term_sems.at[0], term_sems.at[1], (d, peer)
        ).start()
        return carry

    lax.fori_loop(1, n_exp, to_peer, 0)

    for step in range(3):
        for side in range(2):
            chunk = orders[side][step]
            own(side, chunk).wait_recv()
            passed(side, chunk).start()
    for step in range(3, 6):
        for side in range(2):
            own(side, orders[side][step]).wait_recv()
    for copy in locals_:
        copy.wait()
    for step in range(6):
        for side in range(2):
            own(side, orders[side][step]).wait_send()
    for step in range(3):
        for side in range(2):
            passed(side, orders[side][step]).wait()
    take_all(rows_ref, n_exp - 1, row_sems.at[0])
    take_all(rows_out, n_exp - 1, row_sems.at[1])
    take_all(terms_ref, n_exp - 1, term_sems.at[0])
    take_all(terms_out, n_exp - 1, term_sems.at[1])


def return_kernel(
    n_dp, n_exp, rows_ref, sums_ref, rows_out, sums_out, row_sems, self_sems, sum_sems
):
    d = lax.axis_index("dp")
    e = lax.axis_index("expert")

    def small(step):
        peer = (d + step) % n_dp
        return remote(
            sums_ref.at[peer], sums_out.at[d], sum_sems.at[0, step], sum_sems.at[1, step], (peer, e)
        )

    for step in range(1, n_dp):
        small(step).start()
    locals_ = (
        pltpu.make_async_copy(rows_ref.at[e], rows_out.at[e], self_sems.at[0]),
        pltpu.make_async_copy(sums_ref.at[d], sums_out.at[d], self_sems.at[1]),
    )
    for copy in locals_:
        copy.start()

    def to_peer(s, carry):
        peer = (e + (s * STRIDE) % n_exp) % n_exp
        remote(
            rows_ref.at[peer], rows_out.at[e], row_sems.at[0], row_sems.at[1], (d, peer)
        ).start()
        return carry

    lax.fori_loop(1, n_exp, to_peer, 0)
    for copy in locals_:
        copy.wait()
    for step in range(1, n_dp):
        small(step).wait()
    take_all(rows_ref, n_exp - 1, row_sems.at[0])
    take_all(rows_out, n_exp - 1, row_sems.at[1])


def send_all(n_dp, n_exp, rows, terms, gate, up, down):
    def like(array):
        return jax.ShapeDtypeStruct(array.shape, array.dtype)

    def gathered(array):
        return jax.ShapeDtypeStruct((n_dp, *array.shape), array.dtype)

    dma = pltpu.SemaphoreType.DMA
    return pl.pallas_call(
        functools.partial(send_kernel, n_dp, n_exp),
        name="send_all",
        out_shape=(like(rows), like(terms), gathered(gate), gathered(up), gathered(down)),
        in_specs=[pl.BlockSpec(memory_space=pl.ANY)] * 5,
        out_specs=[pl.BlockSpec(memory_space=pl.ANY)] * 5,
        scratch_shapes=[
            dma((2,)),
            dma((2,)),
            dma((5,)),
            dma((2, 6)),
            dma((2, 6)),
            dma((2, 3)),
            dma((2, 3)),
        ],
        compiler_params=pltpu.CompilerParams(has_side_effects=True),
    )(rows, terms, gate, up, down)


def return_all(n_dp, n_exp, rows, sums):
    def like(array):
        return jax.ShapeDtypeStruct(array.shape, array.dtype)

    dma = pltpu.SemaphoreType.DMA
    return pl.pallas_call(
        functools.partial(return_kernel, n_dp, n_exp),
        name="return_all",
        out_shape=(like(rows), like(sums)),
        in_specs=[pl.BlockSpec(memory_space=pl.ANY)] * 2,
        out_specs=[pl.BlockSpec(memory_space=pl.ANY)] * 2,
        scratch_shapes=[dma((2,)), dma((2,)), dma((2, n_dp))],
        compiler_params=pltpu.CompilerParams(has_side_effects=True),
    )(rows, sums)


def arrange(group):
    i = np.arange(group * 16)
    quarter, kind, expert, slot = i // (4 * group), i // (2 * group) % 2, i // 2 % group, i % 2
    move = np.zeros((group * 16, group * 16), np.float32)
    move[i, expert * 16 + quarter * 4 + kind * 2 + slot] = 1.0
    return move


def pack(first, second, unmove, quarter):
    parts = []
    for q in range(4):
        columns = slice(q * quarter, (q + 1) * quarter)
        parts += [first[:, columns], second[:, columns]]
    stacked = jnp.concatenate(parts, axis=0)
    return jnp.dot(unmove, stacked, preferred_element_type=F32).astype(BF16)


def pack_kernel(placing_ref, stacked_ref, unmove_ref, out_ref):
    rows = jnp.dot(placing_ref[...], stacked_ref[...], preferred_element_type=F32).astype(BF16)
    half = rows.shape[0] // 2
    out_ref[...] = pack(rows[:half], rows[half:], unmove_ref[...], out_ref.shape[1])


def pack_rows(group, placing, stacked, unmove):
    count, width = placing.shape[0], stacked.shape[1]
    return pl.pallas_call(
        pack_kernel,
        name="pack_rows",
        grid=(count // (4 * group),),
        out_shape=jax.ShapeDtypeStruct((count * 4, width // 4), BF16),
        in_specs=[
            pl.BlockSpec((4 * group, stacked.shape[0]), lambda i: (i, 0)),
            pl.BlockSpec(stacked.shape, lambda i: (0, 0)),
            pl.BlockSpec(unmove.shape, lambda i: (0, 0)),
        ],
        out_specs=pl.BlockSpec((16 * group, width // 4), lambda i: (i, 0)),
        compiler_params=pltpu.CompilerParams(vmem_limit_bytes=32 << 20),
    )(placing, stacked, unmove)


def expert_kernel(
    group,
    rows_ref,
    move_ref,
    unmove_ref,
    router_ref,
    mine_ref,
    gate_ref,
    up_ref,
    down_ref,
    out_ref,
    sum_ref,
    tok,
    cot,
    grad,
    value,
    total_out,
    total_grad,
):
    step = pl.program_id(0)
    quarter = rows_ref.shape[1]
    block, span = 16 * group, 2 * group
    blocks = rows_ref.shape[0] // block
    transposed = (((1,), (1,)), ((), ()))

    @pl.when(step == 0)
    def _():
        for b in range(blocks):
            moved = jnp.dot(
                move_ref[...], rows_ref[pl.ds(b * block, block), :], preferred_element_type=F32
            ).astype(BF16)
            for q in range(4):
                at = (pl.ds(b * span, span), pl.ds(q * quarter, quarter))
                tok[at] = moved[2 * q * span : (2 * q + 1) * span]
                cot[at] = moved[(2 * q + 1) * span : (2 * q + 2) * span]
        logits = jnp.dot(tok[...], router_ref[...], preferred_element_type=F32)
        gate = jax.nn.sigmoid(jnp.sum(logits * mine_ref[0:1, :], axis=1, keepdims=True))
        value[...] = jnp.broadcast_to(gate, value.shape)
        grad[...] = (ROUTE_SCALE * gate * cot[...].astype(F32)).astype(BF16)

    gate_pre = lax.dot_general(tok[...], gate_ref[...], transposed, preferred_element_type=F32)
    up_pre = lax.dot_general(tok[...], up_ref[...], transposed, preferred_element_type=F32)
    hidden_grad = lax.dot_general(
        grad[...], down_ref[...], transposed, preferred_element_type=F32
    )
    squash = jax.nn.sigmoid(gate_pre)
    active = gate_pre * squash
    hidden = (active * up_pre).astype(BF16)
    gate_grad = (hidden_grad * up_pre * squash * (1.0 + gate_pre * (1.0 - squash))).astype(BF16)
    up_grad = (hidden_grad * active).astype(BF16)
    more_out = jnp.dot(hidden, down_ref[...], preferred_element_type=F32)
    more_grad = jnp.dot(gate_grad, gate_ref[...], preferred_element_type=F32) + jnp.dot(
        up_grad, up_ref[...], preferred_element_type=F32
    )

    @pl.when(step == 0)
    def _():
        total_out[...] = more_out
        total_grad[...] = more_grad

    @pl.when(step > 0)
    def _():
        total_out[...] += more_out
        total_grad[...] += more_grad

    @pl.when(step == pl.num_programs(0) - 1)
    def _():
        gate = value[:, 0:1]
        expert_out = total_out[...].astype(BF16).astype(F32)
        affinity_grad = ROUTE_SCALE * jnp.sum(
            cot[...].astype(F32) * expert_out, axis=1, keepdims=True
        )
        lift = gate * (1.0 - gate) * affinity_grad
        column = lax.dot_general(
            mine_ref[...].astype(BF16), router_ref[...], transposed, preferred_element_type=F32
        )[0:1]
        sum_ref[...] = jnp.broadcast_to(
            jnp.sum(lift * tok[...].astype(F32), axis=0, keepdims=True), sum_ref.shape
        )
        grad[...] = (total_grad[...] + lift * column).astype(BF16)
        tok[...] = (ROUTE_SCALE * gate * expert_out).astype(BF16)
        for b in range(blocks):
            at = pl.ds(b * span, span)
            out_ref[pl.ds(b * block, block), :] = pack(
                grad[at, :], tok[at, :], unmove_ref[...], quarter
            )


def expert_rows(group, rows, move, unmove, router, mine, gate, up, down):
    hidden, width = gate.shape
    tile = 256
    slots = rows.shape[0] // 8

    def whole(array):
        return pl.BlockSpec(array.shape, lambda i: (0,) * array.ndim)

    weight = pl.BlockSpec((tile, width), lambda i: (i, 0))
    summed = jax.ShapeDtypeStruct((8, width), F32)
    return pl.pallas_call(
        functools.partial(expert_kernel, group),
        name="expert_rows",
        grid=(hidden // tile,),
        out_shape=(jax.ShapeDtypeStruct(rows.shape, BF16), summed),
        in_specs=[whole(rows), whole(move), whole(unmove), whole(router), whole(mine)]
        + [weight] * 3,
        out_specs=(whole(rows), whole(summed)),
        scratch_shapes=[
            pltpu.VMEM((slots, width), BF16),
            pltpu.VMEM((slots, width), BF16),
            pltpu.VMEM((slots, width), BF16),
            pltpu.VMEM((slots, 128), F32),
            pltpu.VMEM((slots, width), F32),
            pltpu.VMEM((slots, width), F32),
        ],
        compiler_params=pltpu.CompilerParams(vmem_limit_bytes=58 << 20),
    )(rows, move, unmove, router, mine, gate, up, down)


def home_kernel(group, rows_ref, move_ref, taking_ref, spread_ref, router_ref, routed_ref, token_ref, flat):
    quarter = rows_ref.shape[1]
    block, part = 16 * group, 4 * group
    for b in range(rows_ref.shape[0] // block):
        moved = jnp.dot(
            move_ref[...], rows_ref[pl.ds(b * block, block), :], preferred_element_type=F32
        ).astype(BF16)
        for q in range(4):
            flat[pl.ds(b * part, part), pl.ds(q * quarter, quarter)] = moved[
                q * part : (q + 1) * part
            ]
    home = jnp.dot(taking_ref[...], flat[...], preferred_element_type=F32)
    back = lax.dot_general(
        spread_ref[...], router_ref[...], (((1,), (1,)), ((), ())), preferred_element_type=F32
    )
    tokens = token_ref.shape[0]
    token_ref[...] = (home[:tokens] + back).astype(BF16)
    routed_ref[...] = home[tokens:].astype(BF16)


def home_rows(group, rows, move, taking, spread, router):
    tokens, width = spread.shape[0], router.shape[0]

    def out(count):
        return jax.ShapeDtypeStruct((count, width), BF16)

    return pl.pallas_call(
        functools.partial(home_kernel, group),
        name="home_rows",
        out_shape=(out(taking.shape[0] - tokens), out(tokens)),
        scratch_shapes=[pltpu.VMEM((rows.shape[0] // 4, width), BF16)],
        compiler_params=pltpu.CompilerParams(vmem_limit_bytes=32 << 20),
    )(rows, move, taking, spread, router)


def on_device(n_dp, n_exp, tokens, routes, counts, router, gate_up_weight, down_weight, cotangent):
    members, tok_local = routes.shape
    width = tokens.shape[1]
    experts = router.shape[1]
    per_member = experts // members
    copies = members * tok_local
    tok_total = tok_local * n_dp * n_exp
    half = width // 2
    part = width // n_dp
    slots = experts * CAP
    mine = lax.axis_index("expert")

    router_full = lax.all_gather(router, "dp", axis=0, tiled=True)
    logits = jnp.dot(tokens, router_full, preferred_element_type=F32)
    affinity = jax.nn.sigmoid(logits)
    slope = affinity * (1.0 - affinity)
    dense = lax.dot_general(
        slope.astype(BF16), tokens, (((0,), (0,)), ((), ())), preferred_element_type=F32
    ).astype(BF16)
    spare = jnp.zeros((experts, experts), BF16)
    held = jnp.broadcast_to(counts.astype(BF16), (experts, experts))
    terms = jnp.concatenate([dense[:, :half], held, dense[:, half:], spare], axis=1)
    terms = terms.reshape(experts, 2, half + experts)

    earlier = (
        (routes[:, :, None] == routes[:, None, :])
        & (jnp.arange(tok_local)[None, None, :] < jnp.arange(tok_local)[None, :, None])
    ).astype(jnp.int32)
    rank = jnp.sum(earlier, axis=2)
    owners = routes + per_member * jnp.arange(members, dtype=jnp.int32)[:, None]
    group = min(16, experts)
    move_np = arrange(group)
    move, unmove = jnp.asarray(move_np, BF16), jnp.asarray(move_np.T, BF16)
    first = owners // group * (4 * group) + owners % group * CAP + rank
    second = first + 2 * group
    row_ids = jnp.arange(2 * slots, dtype=jnp.int32)
    token_hits = jnp.any(row_ids[:, None, None] == first[None, :, :], axis=1)
    copy_hits = row_ids[:, None] == second.reshape(1, copies)
    placing = jnp.concatenate([token_hits, copy_hits], axis=1).astype(BF16)
    token_takes = jnp.any(first[:, :, None] == row_ids[None, None, :], axis=0)
    copy_takes = second.reshape(copies, 1) == row_ids[None, :]
    taking = jnp.concatenate([token_takes, copy_takes], axis=0).astype(BF16)
    stacked = jnp.concatenate([tokens, cotangent.reshape(copies, width)], axis=0)
    rows = pack_rows(group, placing, stacked, unmove).reshape(experts, 16, width // 4)

    rows_in, terms_in, gate_full, up_full, down_full = send_all(
        n_dp,
        n_exp,
        rows,
        terms,
        gate_up_weight[0, :, 0, :],
        gate_up_weight[0, :, 1, :],
        down_weight[0],
    )

    is_mine = (jnp.arange(experts, dtype=jnp.int32) == mine).astype(F32)
    results, routed_sum = expert_rows(
        group,
        rows_in.reshape(experts * 16, width // 4),
        move,
        unmove,
        router_full,
        jnp.broadcast_to(is_mine[None, :], (8, experts)),
        gate_full.reshape(-1, width),
        up_full.reshape(-1, width),
        down_full.reshape(-1, width),
    )
    terms_sum = jnp.sum(terms_in.astype(F32), axis=0)
    dense_sum = terms_sum[:, :half].reshape(n_dp, part)
    load = jnp.broadcast_to(terms_sum[:1, half:], (n_dp, experts))
    sums = jnp.concatenate([dense_sum, routed_sum[0].reshape(n_dp, part), load], axis=1)
    short = -sums.shape[1] % 1024
    sums = jnp.pad(sums, ((0, 0), (0, short))).reshape(n_dp, 8, -1)

    results_in, sums_in = return_all(
        n_dp, n_exp, results.reshape(experts, 16, width // 4), sums
    )

    total = jnp.sum(sums_in, axis=0).reshape(-1)
    balance = per_member * total[2 * part : 2 * part + experts] / tok_total
    router_grad = (
        BALANCE * jnp.sum(balance * is_mine) * total[:part] + total[part : 2 * part]
    ) * tok_total ** (-0.5)
    spread = (slope * (BALANCE * balance)[None, :]).astype(BF16)
    routed_out, token_grad = home_rows(
        group,
        results_in.reshape(experts * 16, width // 4),
        move,
        taking,
        spread,
        router_full,
    )
    routed_out = routed_out.reshape(members, tok_local, width)
    return (routed_out, token_grad, router_grad[:, None])


def solution(mesh):
    in_specs = (
        P(("dp", "expert"), None),
        P(None, ("dp", "expert")),
        P(("dp", "expert"), None),
        P("dp", None),
        P("expert", "dp", None, None),
        P("expert", "dp", None),
        P(None, ("dp", "expert"), None),
    )
    out_specs = (P(None, ("dp", "expert"), None), P(("dp", "expert"), None), P("dp", "expert"))
    sizes = (mesh.shape["dp"], mesh.shape["expert"])
    return jax.shard_map(
        functools.partial(on_device, *sizes),
        mesh=mesh,
        in_specs=in_specs,
        out_specs=out_specs,
        check_vma=False,
    )
```

```python
import functools

import jax
import jax.numpy as jnp
import numpy as np
from jax import lax
from jax.experimental import pallas as pl
from jax.experimental.pallas import tpu as pltpu
from jax.sharding import PartitionSpec as P

ROUTE_SCALE = 2.5
BALANCE = 1.0
CAP = 2
STRIDE = 37
MESH = pl.DeviceIdType.MESH
BF16 = jnp.bfloat16
F32 = jnp.float32


def remote(src, dst, send_sem, recv_sem, device):
    return pltpu.make_async_remote_copy(
        src_ref=src,
        dst_ref=dst,
        send_sem=send_sem,
        recv_sem=recv_sem,
        device_id=device,
        device_id_type=MESH,
    )


def take_all(ref, count, sem):
    block = ref.at[pl.ds(0, count)]
    pltpu.make_async_copy(block, block, sem).wait()


def send_rows(n_exp, d, e, source, target, sems):
    def to_peer(s, carry):
        peer = (e + (s * STRIDE) % n_exp) % n_exp
        remote(source.at[peer], target.at[e], sems.at[0], sems.at[1], (d, peer)).start()
        return carry

    lax.fori_loop(1, n_exp, to_peer, 0)


def send_kernel(
    n_dp,
    n_exp,
    placing_ref,
    stacked_ref,
    unmove_ref,
    unterm_ref,
    counts_ref,
    router_ref,
    gate_ref,
    up_ref,
    down_ref,
    rows_out,
    terms_out,
    router_out,
    slope_out,
    gate_out,
    up_out,
    down_out,
    rows,
    terms,
    router_all,
    row_sems,
    term_sems,
    self_sems,
    half_sems,
    swap_sems,
    own_send,
    own_recv,
    pass_send,
    pass_recv,
):
    d = lax.axis_index("dp")
    e = lax.axis_index("expert")
    core = e % 2
    sibling = e + 1 - 2 * core
    sides = ((d + 1) % n_dp, (d + n_dp - 1) % n_dp)
    span = gate_ref.shape[0] // 2
    held = (gate_ref, up_ref, down_ref)
    full = (gate_out, up_out, down_out)

    def piece(refs, shard, chunk):
        ref, part = refs[chunk // 2], pl.ds(chunk % 2 * span, span)
        return ref.at[part] if shard is None else ref.at[shard, part]

    orders = ((0, 1, 2, 3, 4, 5), (3, 4, 5, 0, 1, 2))

    def own(side, chunk):
        return remote(
            piece(held, None, chunk),
            piece(full, d, chunk),
            own_send.at[side, chunk],
            own_recv.at[side, chunk],
            (sides[side], e),
        )

    def passed(side, chunk):
        source = sides[1 - side]
        return remote(
            piece(full, source, chunk),
            piece(full, source, chunk),
            pass_send.at[side, chunk % 3],
            pass_recv.at[side, chunk % 3],
            (sides[side], e),
        )

    def router_half(step):
        return remote(
            router_ref.at[core],
            router_all.at[d, core],
            half_sems.at[0, step],
            half_sems.at[1, step],
            ((d + step) % n_dp, e),
        )

    def router_swap(step):
        shard = (d + n_dp - step) % n_dp
        return remote(
            router_all.at[shard, core],
            router_all.at[shard, core],
            swap_sems.at[0, step],
            swap_sems.at[1, step],
            (d, sibling),
        )

    for step in range(1, n_dp):
        router_half(step).start()
    for step in range(6):
        for side in range(2):
            own(side, orders[side][step]).start()
    own_router = pltpu.make_async_copy(router_ref, router_all.at[d], self_sems.at[5])
    own_router.start()
    locals_ = [
        pltpu.make_async_copy(gate_ref, gate_out.at[d], self_sems.at[0]),
        pltpu.make_async_copy(up_ref, up_out.at[d], self_sems.at[1]),
        pltpu.make_async_copy(down_ref, down_out.at[d], self_sems.at[2]),
    ]
    for copy in locals_:
        copy.start()

    group = unmove_ref.shape[0] // 16
    quarter = rows.shape[2]
    for b in range(n_exp // group):
        placed = jnp.dot(
            placing_ref[pl.ds(b * 4 * group, 4 * group), :],
            stacked_ref[...],
            preferred_element_type=F32,
        ).astype(BF16)
        rows[pl.ds(b * group, group)] = pack(
            placed[: 2 * group], placed[2 * group :], unmove_ref[...], quarter
        ).reshape(group, 16, quarter)
    send_rows(n_exp, d, e, rows, rows_out, row_sems)
    locals_.append(pltpu.make_async_copy(rows.at[e], rows_out.at[e], self_sems.at[3]))
    locals_[-1].start()

    for step in range(1, n_dp):
        router_half(step).wait_recv()
        router_swap(step).start()
    own_router.wait()
    for step in range(1, n_dp):
        router_swap(step).wait_recv()
    router = router_all[...].reshape(router_out.shape)
    router_out[...] = router
    tokens = stacked_ref[pl.ds(0, slope_out.shape[0]), :]
    affinity = jax.nn.sigmoid(jnp.dot(tokens, router, preferred_element_type=F32))
    slope = affinity * (1.0 - affinity)
    slope_out[...] = slope
    dense = lax.dot_general(
        slope.astype(BF16), tokens, (((0,), (0,)), ((), ())), preferred_element_type=F32
    ).astype(BF16)
    lanes = terms.shape[2]
    parts = tokens.shape[1] // lanes
    blank = jnp.zeros(((15 - parts) * group, lanes), BF16)
    for b in range(n_exp // group):
        block = [
            dense[b * group : (b + 1) * group, r * lanes : (r + 1) * lanes] for r in range(parts)
        ]
        stack = jnp.concatenate([*block, counts_ref[...], blank], axis=0)
        moved = jnp.dot(unterm_ref[...], stack, preferred_element_type=F32).astype(BF16)
        terms[pl.ds(b * group, group)] = moved.reshape(group, 16, lanes)
    send_rows(n_exp, d, e, terms, terms_out, term_sems)
    locals_.append(pltpu.make_async_copy(terms.at[e], terms_out.at[e], self_sems.at[4]))
    locals_[-1].start()

    for step in range(3):
        for side in range(2):
            chunk = orders[side][step]
            own(side, chunk).wait_recv()
            passed(side, chunk).start()
    for step in range(3, 6):
        for side in range(2):
            own(side, orders[side][step]).wait_recv()
    for copy in locals_:
        copy.wait()
    for step in range(1, n_dp):
        router_half(step).wait_send()
        router_swap(step).wait_send()
    for step in range(6):
        for side in range(2):
            own(side, orders[side][step]).wait_send()
    for step in range(3):
        for side in range(2):
            passed(side, orders[side][step]).wait()
    take_all(rows, n_exp - 1, row_sems.at[0])
    take_all(rows_out, n_exp - 1, row_sems.at[1])
    take_all(terms, n_exp - 1, term_sems.at[0])
    take_all(terms_out, n_exp - 1, term_sems.at[1])


def send_all(n_dp, n_exp, tokens, placing, stacked, unmove, unterm, counts, router, gate, up, down):
    width = stacked.shape[1]
    experts = placing.shape[0] // 4

    def gathered(array):
        return jax.ShapeDtypeStruct((n_dp, *array.shape), array.dtype)

    dma = pltpu.SemaphoreType.DMA
    hbm, vmem = pl.BlockSpec(memory_space=pl.ANY), pl.BlockSpec(memory_space=pltpu.VMEM)
    rows = (experts, 16, width // 4)
    terms = (experts, 16, 256)
    return pl.pallas_call(
        functools.partial(send_kernel, n_dp, n_exp),
        name="send_all",
        out_shape=(
            jax.ShapeDtypeStruct(rows, BF16),
            jax.ShapeDtypeStruct(terms, BF16),
            jax.ShapeDtypeStruct((width, experts), BF16),
            jax.ShapeDtypeStruct((tokens, experts), F32),
            gathered(gate),
            gathered(up),
            gathered(down),
        ),
        in_specs=[vmem] * 6 + [hbm] * 3,
        out_specs=[hbm, hbm, vmem, vmem, hbm, hbm, hbm],
        scratch_shapes=[
            pltpu.VMEM(rows, BF16),
            pltpu.VMEM(terms, BF16),
            pltpu.VMEM((n_dp, *router.shape), BF16),
            dma((2,)),
            dma((2,)),
            dma((6,)),
            dma((2, n_dp)),
            dma((2, n_dp)),
            dma((2, 6)),
            dma((2, 6)),
            dma((2, 3)),
            dma((2, 3)),
        ],
        compiler_params=pltpu.CompilerParams(
            has_side_effects=True, vmem_limit_bytes=40 << 20
        ),
    )(placing, stacked, unmove, unterm, counts, router, gate, up, down)


def arrange(group):
    i = np.arange(group * 16)
    quarter, kind, expert, slot = i // (4 * group), i // (2 * group) % 2, i // 2 % group, i % 2
    move = np.zeros((group * 16, group * 16), np.float32)
    move[i, expert * 16 + quarter * 4 + kind * 2 + slot] = 1.0
    return move


def arrange_terms(group):
    i = np.arange(group * 16)
    move = np.zeros((group * 16, group * 16), np.float32)
    move[i, i % 16 * group + i // 16] = 1.0
    return move


def pack(first, second, unmove, quarter):
    parts = []
    for q in range(4):
        columns = slice(q * quarter, (q + 1) * quarter)
        parts += [first[:, columns], second[:, columns]]
    stacked = jnp.concatenate(parts, axis=0)
    return jnp.dot(unmove, stacked, preferred_element_type=F32).astype(BF16)


def expert_kernel(
    n_dp,
    n_exp,
    group,
    per_token,
    rows_ref,
    move_ref,
    unmove_ref,
    router_ref,
    mine_ref,
    terms_ref,
    slope_ref,
    taking_ref,
    gate_ref,
    up_ref,
    down_ref,
    routed_ref,
    token_ref,
    dense_ref,
    sum_ref,
    tok,
    cot,
    grad,
    value,
    total_out,
    total_grad,
    back,
    land,
    flat,
    dense,
    dense_land,
    lifted,
    lifted_land,
    row_sems,
    self_sems,
    dense_sems,
    lifted_sems,
):
    d = lax.axis_index("dp")
    e = lax.axis_index("expert")
    step = pl.program_id(0)
    quarter = rows_ref.shape[1]
    block, span = 16 * group, 2 * group
    blocks = rows_ref.shape[0] // block
    transposed = (((1,), (1,)), ((), ()))

    @pl.when(step == 0)
    def _():
        for b in range(blocks):
            moved = jnp.dot(
                move_ref[...], rows_ref[pl.ds(b * block, block), :], preferred_element_type=F32
            ).astype(BF16)
            for q in range(4):
                at = (pl.ds(b * span, span), pl.ds(q * quarter, quarter))
                tok[at] = moved[2 * q * span : (2 * q + 1) * span]
                cot[at] = moved[(2 * q + 1) * span : (2 * q + 2) * span]
        logits = jnp.dot(tok[...], router_ref[...], preferred_element_type=F32)
        gate = jax.nn.sigmoid(jnp.sum(logits * mine_ref[0:1, :], axis=1, keepdims=True))
        value[...] = jnp.broadcast_to(gate, value.shape)
        grad[...] = (ROUTE_SCALE * gate * cot[...].astype(F32)).astype(BF16)

    gate_pre = lax.dot_general(tok[...], gate_ref[...], transposed, preferred_element_type=F32)
    up_pre = lax.dot_general(tok[...], up_ref[...], transposed, preferred_element_type=F32)
    hidden_grad = lax.dot_general(
        grad[...], down_ref[...], transposed, preferred_element_type=F32
    )
    squash = jax.nn.sigmoid(gate_pre)
    active = gate_pre * squash
    hidden = (active * up_pre).astype(BF16)
    gate_grad = (hidden_grad * up_pre * squash * (1.0 + gate_pre * (1.0 - squash))).astype(BF16)
    up_grad = (hidden_grad * active).astype(BF16)
    more_out = jnp.dot(hidden, down_ref[...], preferred_element_type=F32)
    more_grad = jnp.dot(gate_grad, gate_ref[...], preferred_element_type=F32) + jnp.dot(
        up_grad, up_ref[...], preferred_element_type=F32
    )

    @pl.when(step == 0)
    def _():
        total_out[...] = more_out
        total_grad[...] = more_grad

    @pl.when(step > 0)
    def _():
        total_out[...] += more_out
        total_grad[...] += more_grad

    @pl.when(step == pl.num_programs(0) - 1)
    def _():
        gate = value[:, 0:1]
        expert_out = total_out[...].astype(BF16).astype(F32)
        affinity_grad = ROUTE_SCALE * jnp.sum(
            cot[...].astype(F32) * expert_out, axis=1, keepdims=True
        )
        lift = gate * (1.0 - gate) * affinity_grad
        column = lax.dot_general(
            mine_ref[...].astype(BF16), router_ref[...], transposed, preferred_element_type=F32
        )[0:1]
        lifted[...] = jnp.broadcast_to(
            jnp.sum(lift * tok[...].astype(F32), axis=0, keepdims=True), lifted.shape
        )
        dense[...] = jnp.sum(terms_ref[...].astype(F32), axis=0)

        def small(shift, ref, target, sems):
            return remote(
                ref,
                target.at[d],
                sems.at[0, shift],
                sems.at[1, shift],
                ((d + shift) % n_dp, e),
            )

        smalls = []
        for shift in range(1, n_dp):
            smalls.append(small(shift, dense, dense_land, dense_sems))
            smalls.append(small(shift, lifted, lifted_land, lifted_sems))
        for copy in smalls:
            copy.start()
        grad[...] = (total_grad[...] + lift * column).astype(BF16)
        tok[...] = (ROUTE_SCALE * gate * expert_out).astype(BF16)
        for b in range(blocks):
            at = pl.ds(b * span, span)
            back[pl.ds(b * group, group)] = pack(
                grad[at, :], tok[at, :], unmove_ref[...], quarter
            ).reshape(group, 16, quarter)
        send_rows(n_exp, d, e, back, land, row_sems)
        locals_ = (
            pltpu.make_async_copy(back.at[e], land.at[e], self_sems.at[0]),
            pltpu.make_async_copy(dense, dense_land.at[d], self_sems.at[1]),
            pltpu.make_async_copy(lifted, lifted_land.at[d], self_sems.at[2]),
        )
        for copy in locals_:
            copy.start()
        for copy in locals_:
            copy.wait()
        for copy in smalls:
            copy.wait()
        sum_ref[...] = jnp.sum(lifted_land[...], axis=0)
        all_dense = jnp.sum(dense_land[...], axis=0)
        dense_ref[...] = all_dense
        parts = tok.shape[1] // all_dense.shape[1]
        load = all_dense[parts : parts + 1, : slope_ref.shape[1]]
        spread = (slope_ref[...] * (BALANCE * (per_token * load))).astype(BF16)
        router_back = lax.dot_general(
            spread, router_ref[...], transposed, preferred_element_type=F32
        )

        take_all(back, n_exp - 1, row_sems.at[0])
        take_all(land, n_exp - 1, row_sems.at[1])
        part = 4 * group
        for b in range(blocks):
            moved = jnp.dot(
                move_ref[...],
                land[pl.ds(b * group, group)].reshape(block, quarter),
                preferred_element_type=F32,
            ).astype(BF16)
            for q in range(4):
                flat[pl.ds(b * part, part), pl.ds(q * quarter, quarter)] = moved[
                    q * part : (q + 1) * part
                ]
        home = jnp.dot(taking_ref[...], flat[...], preferred_element_type=F32)
        tokens = token_ref.shape[0]
        token_ref[...] = (home[:tokens] + router_back).astype(BF16)
        routed_ref[...] = home[tokens:].astype(BF16)


def expert_rows(
    n_dp, n_exp, group, per_token, rows, move, unmove, router, mine, terms, slope, taking, gate, up, down
):
    hidden, width = gate.shape
    tile = 256
    slots = rows.shape[0] // 8
    tokens = slope.shape[0]

    def whole(array):
        return pl.BlockSpec(array.shape, lambda i: (0,) * len(array.shape))

    def out(*shape, kind=BF16):
        return jax.ShapeDtypeStruct(shape, kind)

    weight = pl.BlockSpec((tile, width), lambda i: (i, 0))
    outs = (
        out(taking.shape[0] - tokens, width),
        out(tokens, width),
        out(*terms.shape[1:], kind=F32),
        out(8, width, kind=F32),
    )
    wholes = (rows, move, unmove, router, mine, terms, slope, taking)
    message = pltpu.VMEM((slots // CAP, 16, width // 4), BF16)
    dma = pltpu.SemaphoreType.DMA
    return pl.pallas_call(
        functools.partial(expert_kernel, n_dp, n_exp, group, per_token),
        name="expert_rows",
        grid=(hidden // tile,),
        out_shape=outs,
        in_specs=[whole(array) for array in wholes] + [weight] * 3,
        out_specs=[whole(array) for array in outs],
        scratch_shapes=[
            pltpu.VMEM((slots, width), BF16),
            pltpu.VMEM((slots, width), BF16),
            pltpu.VMEM((slots, width), BF16),
            pltpu.VMEM((slots, 128), F32),
            pltpu.VMEM((slots, width), F32),
            pltpu.VMEM((slots, width), F32),
            message,
            message,
            pltpu.VMEM((2 * slots, width), BF16),
            pltpu.VMEM(terms.shape[1:], F32),
            pltpu.VMEM((n_dp, *terms.shape[1:]), F32),
            pltpu.VMEM((8, width), F32),
            pltpu.VMEM((n_dp, 8, width), F32),
            dma((2,)),
            dma((3,)),
            dma((2, n_dp)),
            dma((2, n_dp)),
        ],
        compiler_params=pltpu.CompilerParams(
            has_side_effects=True, vmem_limit_bytes=58 << 20
        ),
    )(*wholes, gate, up, down)


def on_device(n_dp, n_exp, tokens, routes, counts, router, gate_up_weight, down_weight, cotangent):
    members, tok_local = routes.shape
    width = tokens.shape[1]
    experts = router.shape[1]
    per_member = experts // members
    copies = members * tok_local
    tok_total = tok_local * n_dp * n_exp
    part = width // n_dp
    slots = experts * CAP
    d, mine = lax.axis_index("dp"), lax.axis_index("expert")

    earlier = (
        (routes[:, :, None] == routes[:, None, :])
        & (jnp.arange(tok_local)[None, None, :] < jnp.arange(tok_local)[None, :, None])
    ).astype(jnp.int32)
    rank = jnp.sum(earlier, axis=2)
    owners = routes + per_member * jnp.arange(members, dtype=jnp.int32)[:, None]
    group = min(16, experts)
    move_np = arrange(group)
    move, unmove = jnp.asarray(move_np, BF16), jnp.asarray(move_np.T, BF16)
    first = owners // group * (4 * group) + owners % group * CAP + rank
    second = first + 2 * group
    row_ids = jnp.arange(2 * slots, dtype=jnp.int32)
    token_hits = jnp.any(row_ids[:, None, None] == first[None, :, :], axis=1)
    copy_hits = row_ids[:, None] == second.reshape(1, copies)
    placing = jnp.concatenate([token_hits, copy_hits], axis=1).astype(BF16)
    token_takes = jnp.any(first[:, :, None] == row_ids[None, None, :], axis=0)
    copy_takes = second.reshape(copies, 1) == row_ids[None, :]
    taking = jnp.concatenate([token_takes, copy_takes], axis=0).astype(BF16)
    stacked = jnp.concatenate([tokens, cotangent.reshape(copies, width)], axis=0)
    held = jnp.pad(counts.astype(BF16), ((0, 0), (0, 256 - experts)))
    rows_in, terms_in, router_full, slope, gate_full, up_full, down_full = send_all(
        n_dp,
        n_exp,
        tok_local,
        placing,
        stacked,
        unmove,
        jnp.asarray(arrange_terms(group), BF16),
        jnp.broadcast_to(held, (group, 256)),
        router.reshape(2, part // 2, experts),
        gate_up_weight[0, :, 0, :],
        gate_up_weight[0, :, 1, :],
        down_weight[0],
    )

    is_mine = (jnp.arange(experts, dtype=jnp.int32) == mine).astype(F32)
    routed_out, token_grad, dense_sum, routed_sum = expert_rows(
        n_dp,
        n_exp,
        group,
        per_member / tok_total,
        rows_in.reshape(experts * 16, width // 4),
        move,
        unmove,
        router_full,
        jnp.broadcast_to(is_mine[None, :], (8, experts)),
        terms_in,
        slope,
        taking,
        gate_full.reshape(-1, width),
        up_full.reshape(-1, width),
        down_full.reshape(-1, width),
    )
    routed_out = routed_out.reshape(members, tok_local, width)
    load = dense_sum[width // 256, :experts]
    balance = per_member * jnp.sum(load * is_mine) / tok_total
    grad = BALANCE * balance * dense_sum.reshape(-1)[:width] + routed_sum[0]
    router_grad = lax.dynamic_slice(grad, (d * part,), (part,)) * tok_total ** (-0.5)
    return (routed_out, token_grad, router_grad[:, None])


def solution(mesh):
    in_specs = (
        P(("dp", "expert"), None),
        P(None, ("dp", "expert")),
        P(("dp", "expert"), None),
        P("dp", None),
        P("expert", "dp", None, None),
        P("expert", "dp", None),
        P(None, ("dp", "expert"), None),
    )
    out_specs = (P(None, ("dp", "expert"), None), P(("dp", "expert"), None), P("dp", "expert"))
    sizes = (mesh.shape["dp"], mesh.shape["expert"])
    return jax.shard_map(
        functools.partial(on_device, *sizes),
        mesh=mesh,
        in_specs=in_specs,
        out_specs=out_specs,
        check_vma=False,
    )
```

```python
import functools

import jax
import jax.numpy as jnp
import numpy as np
from jax import lax
from jax.experimental import pallas as pl
from jax.experimental.pallas import tpu as pltpu
from jax.sharding import PartitionSpec as P

ROUTE_SCALE = 2.5
BALANCE = 1.0
CAP = 2
STRIDE = 37
MESH = pl.DeviceIdType.MESH
BF16 = jnp.bfloat16
F32 = jnp.float32


def remote(src, dst, send_sem, recv_sem, device):
    return pltpu.make_async_remote_copy(
        src_ref=src,
        dst_ref=dst,
        send_sem=send_sem,
        recv_sem=recv_sem,
        device_id=device,
        device_id_type=MESH,
    )


def take_all(ref, count, sem):
    block = ref.at[pl.ds(0, count)]
    pltpu.make_async_copy(block, block, sem).wait()


def send_rows(n_exp, d, e, source, target, sems):
    def to_peer(s, carry):
        peer = (e + (s * STRIDE) % n_exp) % n_exp
        remote(source.at[peer], target.at[e], sems.at[0], sems.at[1], (d, peer)).start()
        return carry

    lax.fori_loop(1, n_exp, to_peer, 0)


def arrange(group):
    i = np.arange(group * 16)
    quarter, kind, expert, slot = i // (4 * group), i // (2 * group) % 2, i // 2 % group, i % 2
    move = np.zeros((group * 16, group * 16), np.float32)
    move[i, expert * 16 + quarter * 4 + kind * 2 + slot] = 1.0
    return move


def arrange_terms(group):
    i = np.arange(group * 16)
    move = np.zeros((group * 16, group * 16), np.float32)
    move[i, i % 16 * group + i // 16] = 1.0
    return move


def pack(first, second, unmove, quarter):
    parts = []
    for q in range(4):
        columns = slice(q * quarter, (q + 1) * quarter)
        parts += [first[:, columns], second[:, columns]]
    stacked = jnp.concatenate(parts, axis=0)
    return jnp.dot(unmove, stacked, preferred_element_type=F32).astype(BF16)


def layer_kernel(
    n_dp,
    n_exp,
    per_token,
    placing_ref,
    stacked_ref,
    move_ref,
    unmove_ref,
    unterm_ref,
    counts_ref,
    router_ref,
    mine_ref,
    gate_ref,
    up_ref,
    down_ref,
    routed_ref,
    token_ref,
    dense_ref,
    sum_ref,
    tok,
    cot,
    grad,
    value,
    total_out,
    total_grad,
    rows,
    rows_in,
    terms,
    terms_in,
    router_all,
    slope_s,
    gate_all,
    up_all,
    down_all,
    back,
    land,
    flat,
    dense_s,
    dense_land,
    lifted,
    lifted_land,
    row_sems,
    term_sems,
    self_sems,
    half_sems,
    swap_sems,
    own_send,
    own_recv,
    pass_send,
    pass_recv,
    back_sems,
    back_self,
    dense_sems,
    lifted_sems,
):
    d = lax.axis_index("dp")
    e = lax.axis_index("expert")
    core = e % 2
    sibling = e + 1 - 2 * core
    sides = ((d + 1) % n_dp, (d + n_dp - 1) % n_dp)
    span = gate_ref.shape[0] // 2
    held = (gate_ref, up_ref, down_ref)
    full = (gate_all, up_all, down_all)

    def piece(refs, shard, chunk):
        ref, part = refs[chunk // 2], pl.ds(chunk % 2 * span, span)
        return ref.at[part] if shard is None else ref.at[shard, part]

    orders = ((0, 1, 2, 3, 4, 5), (3, 4, 5, 0, 1, 2))

    def own(side, chunk):
        return remote(
            piece(held, None, chunk),
            piece(full, d, chunk),
            own_send.at[side, chunk],
            own_recv.at[side, chunk],
            (sides[side], e),
        )

    def passed(side, chunk):
        source = sides[1 - side]
        return remote(
            piece(full, source, chunk),
            piece(full, source, chunk),
            pass_send.at[side, chunk % 3],
            pass_recv.at[side, chunk % 3],
            (sides[side], e),
        )

    def router_half(step):
        return remote(
            router_ref.at[core],
            router_all.at[d, core],
            half_sems.at[0, step],
            half_sems.at[1, step],
            ((d + step) % n_dp, e),
        )

    def router_swap(step):
        shard = (d + n_dp - step) % n_dp
        return remote(
            router_all.at[shard, core],
            router_all.at[shard, core],
            swap_sems.at[0, step],
            swap_sems.at[1, step],
            (d, sibling),
        )

    for step in range(1, n_dp):
        router_half(step).start()
    for step in range(6):
        for side in range(2):
            own(side, orders[side][step]).start()
    own_router = pltpu.make_async_copy(router_ref, router_all.at[d], self_sems.at[5])
    own_router.start()
    locals_ = [
        pltpu.make_async_copy(gate_ref, gate_all.at[d], self_sems.at[0]),
        pltpu.make_async_copy(up_ref, up_all.at[d], self_sems.at[1]),
        pltpu.make_async_copy(down_ref, down_all.at[d], self_sems.at[2]),
    ]
    for copy in locals_:
        copy.start()

    group = unmove_ref.shape[0] // 16
    quarter = rows.shape[2]
    for b in range(n_exp // group):
        placed = jnp.dot(
            placing_ref[pl.ds(b * 4 * group, 4 * group), :],
            stacked_ref[...],
            preferred_element_type=F32,
        ).astype(BF16)
        rows[pl.ds(b * group, group)] = pack(
            placed[: 2 * group], placed[2 * group :], unmove_ref[...], quarter
        ).reshape(group, 16, quarter)
    send_rows(n_exp, d, e, rows, rows_in, row_sems)
    locals_.append(pltpu.make_async_copy(rows.at[e], rows_in.at[e], self_sems.at[3]))
    locals_[-1].start()

    for step in range(1, n_dp):
        router_half(step).wait_recv()
        router_swap(step).start()
    own_router.wait()
    for step in range(1, n_dp):
        router_swap(step).wait_recv()
    router = router_all[...].reshape(stacked_ref.shape[1], n_exp)
    tokens = stacked_ref[pl.ds(0, slope_s.shape[0]), :]
    affinity = jax.nn.sigmoid(jnp.dot(tokens, router, preferred_element_type=F32))
    slope = affinity * (1.0 - affinity)
    slope_s[...] = slope
    dense = lax.dot_general(
        slope.astype(BF16), tokens, (((0,), (0,)), ((), ())), preferred_element_type=F32
    ).astype(BF16)
    lanes = terms.shape[2]
    parts = tokens.shape[1] // lanes
    blank = jnp.zeros(((15 - parts) * group, lanes), BF16)
    for b in range(n_exp // group):
        block = [
            dense[b * group : (b + 1) * group, r * lanes : (r + 1) * lanes] for r in range(parts)
        ]
        stack = jnp.concatenate([*block, counts_ref[...], blank], axis=0)
        moved = jnp.dot(unterm_ref[...], stack, preferred_element_type=F32).astype(BF16)
        terms[pl.ds(b * group, group)] = moved.reshape(group, 16, lanes)
    send_rows(n_exp, d, e, terms, terms_in, term_sems)
    locals_.append(pltpu.make_async_copy(terms.at[e], terms_in.at[e], self_sems.at[4]))
    locals_[-1].start()

    for step in range(3):
        for side in range(2):
            chunk = orders[side][step]
            own(side, chunk).wait_recv()
            passed(side, chunk).start()

    transposed = (((1,), (1,)), ((), ()))
    block, part, two = 16 * group, 4 * group, 2 * group
    blocks = n_exp // group
    for copy in locals_:
        copy.wait()
    take_all(rows_in, n_exp - 1, row_sems.at[1])
    for b in range(blocks):
        moved = jnp.dot(
            move_ref[...],
            rows_in[pl.ds(b * group, group)].reshape(block, quarter),
            preferred_element_type=F32,
        ).astype(BF16)
        for q in range(4):
            at = (pl.ds(b * two, two), pl.ds(q * quarter, quarter))
            tok[at] = moved[2 * q * two : (2 * q + 1) * two]
            cot[at] = moved[(2 * q + 1) * two : (2 * q + 2) * two]
    logits = jnp.dot(tok[...], router, preferred_element_type=F32)
    gate = jax.nn.sigmoid(jnp.sum(logits * mine_ref[0:1, :], axis=1, keepdims=True))
    value[...] = jnp.broadcast_to(gate, value.shape)
    grad[...] = (ROUTE_SCALE * gate * cot[...].astype(F32)).astype(BF16)

    def expert_part(shard, first):
        gate_w, up_w, down_w = gate_all.at[shard], up_all.at[shard], down_all.at[shard]
        gate_pre = lax.dot_general(tok[...], gate_w[...], transposed, preferred_element_type=F32)
        up_pre = lax.dot_general(tok[...], up_w[...], transposed, preferred_element_type=F32)
        hidden_grad = lax.dot_general(
            grad[...], down_w[...], transposed, preferred_element_type=F32
        )
        squash = jax.nn.sigmoid(gate_pre)
        active = gate_pre * squash
        hidden = (active * up_pre).astype(BF16)
        gate_grad = (hidden_grad * up_pre * squash * (1.0 + gate_pre * (1.0 - squash))).astype(BF16)
        up_grad = (hidden_grad * active).astype(BF16)
        more_out = jnp.dot(hidden, down_w[...], preferred_element_type=F32)
        more_grad = jnp.dot(gate_grad, gate_w[...], preferred_element_type=F32) + jnp.dot(
            up_grad, up_w[...], preferred_element_type=F32
        )
        if first:
            total_out[...] = more_out
            total_grad[...] = more_grad
        else:
            total_out[...] += more_out
            total_grad[...] += more_grad

    expert_part(d, True)
    for side in range(2):
        for step in range(3, 6):
            own(side, orders[side][step]).wait_recv()
        expert_part(sides[1 - side], False)
    take_all(terms_in, n_exp - 1, term_sems.at[1])
    dense_s[...] = jnp.sum(terms_in[...].astype(F32), axis=0)
    for step in range(3):
        for side in range(2):
            passed(side, orders[side][step]).wait_recv()
    expert_part((d + 2) % n_dp, False)

    gate = value[:, 0:1]
    expert_out = total_out[...].astype(BF16).astype(F32)
    affinity_grad = ROUTE_SCALE * jnp.sum(
        cot[...].astype(F32) * expert_out, axis=1, keepdims=True
    )
    lift = gate * (1.0 - gate) * affinity_grad
    column = lax.dot_general(
        mine_ref[...].astype(BF16), router, transposed, preferred_element_type=F32
    )[0:1]
    lifted[...] = jnp.broadcast_to(
        jnp.sum(lift * tok[...].astype(F32), axis=0, keepdims=True), lifted.shape
    )

    def small(shift, ref, target, sems):
        return remote(
            ref,
            target.at[d],
            sems.at[0, shift],
            sems.at[1, shift],
            ((d + shift) % n_dp, e),
        )

    smalls = []
    for shift in range(1, n_dp):
        smalls.append(small(shift, dense_s, dense_land, dense_sems))
        smalls.append(small(shift, lifted, lifted_land, lifted_sems))
    for copy in smalls:
        copy.start()
    grad[...] = (total_grad[...] + lift * column).astype(BF16)
    tok[...] = (ROUTE_SCALE * gate * expert_out).astype(BF16)
    for b in range(blocks):
        at = pl.ds(b * two, two)
        back[pl.ds(b * group, group)] = pack(
            grad[at, :], tok[at, :], unmove_ref[...], quarter
        ).reshape(group, 16, quarter)
    send_rows(n_exp, d, e, back, land, back_sems)
    returns = (
        pltpu.make_async_copy(back.at[e], land.at[e], back_self.at[0]),
        pltpu.make_async_copy(dense_s, dense_land.at[d], back_self.at[1]),
        pltpu.make_async_copy(lifted, lifted_land.at[d], back_self.at[2]),
    )
    for copy in returns:
        copy.start()
    for copy in returns:
        copy.wait()
    for copy in smalls:
        copy.wait()
    sum_ref[...] = jnp.sum(lifted_land[...], axis=0)
    all_dense = jnp.sum(dense_land[...], axis=0)
    dense_ref[...] = all_dense
    parts = tok.shape[1] // all_dense.shape[1]
    load = all_dense[parts : parts + 1, : slope_s.shape[1]]
    spread = (slope_s[...] * (BALANCE * (per_token * load))).astype(BF16)
    router_back = lax.dot_general(
        spread, router, transposed, preferred_element_type=F32
    )

    take_all(back, n_exp - 1, back_sems.at[0])
    take_all(land, n_exp - 1, back_sems.at[1])
    for b in range(blocks):
        moved = jnp.dot(
            move_ref[...],
            land[pl.ds(b * group, group)].reshape(block, quarter),
            preferred_element_type=F32,
        ).astype(BF16)
        for q in range(4):
            flat[pl.ds(b * part, part), pl.ds(q * quarter, quarter)] = moved[
                q * part : (q + 1) * part
            ]
    home = lax.dot_general(
        placing_ref[...], flat[...], (((0,), (0,)), ((), ())), preferred_element_type=F32
    )
    count = token_ref.shape[0]
    token_ref[...] = (home[:count] + router_back).astype(BF16)
    routed_ref[...] = home[count:].astype(BF16)

    for step in range(1, n_dp):
        router_half(step).wait_send()
        router_swap(step).wait_send()
    for step in range(6):
        for side in range(2):
            own(side, orders[side][step]).wait_send()
    for step in range(3):
        for side in range(2):
            passed(side, orders[side][step]).wait_send()
    take_all(rows, n_exp - 1, row_sems.at[0])
    take_all(terms, n_exp - 1, term_sems.at[0])


def layer(n_dp, n_exp, tokens, per_token, wholes, weights):
    placing, stacked = wholes[:2]
    width = stacked.shape[1]
    slots = placing.shape[0] // 2
    hidden = weights[0].shape[0]

    def out(*shape, kind=BF16):
        return jax.ShapeDtypeStruct(shape, kind)

    def vmem(*shape, kind=BF16):
        return pltpu.VMEM(shape, kind)

    message = vmem(n_exp, 16, width // 4)
    terms = vmem(n_exp, 16, 256)
    gathered = vmem(n_dp, hidden, width)
    dma = pltpu.SemaphoreType.DMA
    return pl.pallas_call(
        functools.partial(layer_kernel, n_dp, n_exp, per_token),
        name="layer",
        out_shape=(
            out(stacked.shape[0] - tokens, width),
            out(tokens, width),
            out(16, 256, kind=F32),
            out(8, width, kind=F32),
        ),
        in_specs=[pl.BlockSpec(memory_space=pltpu.VMEM)] * 8
        + [pl.BlockSpec(memory_space=pl.ANY)] * 3,
        out_specs=[pl.BlockSpec(memory_space=pltpu.VMEM)] * 4,
        scratch_shapes=[
            *[vmem(slots, width)] * 3,
            vmem(slots, 128, kind=F32),
            *[vmem(slots, width, kind=F32)] * 2,
            *[message] * 2,
            *[terms] * 2,
            vmem(n_dp, *wholes[6].shape),
            vmem(tokens, n_exp, kind=F32),
            *[gathered] * 3,
            *[message] * 2,
            vmem(2 * slots, width),
            vmem(16, 256, kind=F32),
            vmem(n_dp, 16, 256, kind=F32),
            vmem(8, width, kind=F32),
            vmem(n_dp, 8, width, kind=F32),
            dma((2,)),
            dma((2,)),
            dma((6,)),
            dma((2, n_dp)),
            dma((2, n_dp)),
            dma((2, 6)),
            dma((2, 6)),
            dma((2, 3)),
            dma((2, 3)),
            dma((2,)),
            dma((3,)),
            dma((2, n_dp)),
            dma((2, n_dp)),
        ],
        compiler_params=pltpu.CompilerParams(
            has_side_effects=True, vmem_limit_bytes=60 << 20
        ),
    )(*wholes, *weights)


def on_device(n_dp, n_exp, tokens, routes, counts, router, gate_up_weight, down_weight, cotangent):
    members, tok_local = routes.shape
    width = tokens.shape[1]
    experts = router.shape[1]
    per_member = experts // members
    copies = members * tok_local
    tok_total = tok_local * n_dp * n_exp
    part = width // n_dp
    slots = experts * CAP
    d, mine = lax.axis_index("dp"), lax.axis_index("expert")

    earlier = (
        (routes[:, :, None] == routes[:, None, :])
        & (jnp.arange(tok_local)[None, None, :] < jnp.arange(tok_local)[None, :, None])
    ).astype(jnp.int32)
    rank = jnp.sum(earlier, axis=2)
    owners = routes + per_member * jnp.arange(members, dtype=jnp.int32)[:, None]
    group = min(16, experts)
    move_np = arrange(group)
    move, unmove = jnp.asarray(move_np, BF16), jnp.asarray(move_np.T, BF16)
    first = owners // group * (4 * group) + owners % group * CAP + rank
    second = first + 2 * group
    row_ids = jnp.arange(2 * slots, dtype=jnp.int32)
    token_hits = jnp.any(row_ids[:, None, None] == first[None, :, :], axis=1)
    copy_hits = row_ids[:, None] == second.reshape(1, copies)
    placing = jnp.concatenate([token_hits, copy_hits], axis=1).astype(BF16)
    stacked = jnp.concatenate([tokens, cotangent.reshape(copies, width)], axis=0)
    held = jnp.pad(counts.astype(BF16), ((0, 0), (0, 256 - experts)))
    is_mine = (jnp.arange(experts, dtype=jnp.int32) == mine).astype(F32)
    wholes = (
        placing,
        stacked,
        move,
        unmove,
        jnp.asarray(arrange_terms(group), BF16),
        jnp.broadcast_to(held, (group, 256)),
        router.reshape(2, part // 2, experts),
        jnp.broadcast_to(is_mine[None, :], (8, experts)),
    )
    weights = (gate_up_weight[0, :, 0, :], gate_up_weight[0, :, 1, :], down_weight[0])
    routed_out, token_grad, dense_sum, routed_sum = layer(
        n_dp, n_exp, tok_local, per_member / tok_total, wholes, weights
    )
    routed_out = routed_out.reshape(members, tok_local, width)
    load = dense_sum[width // 256, :experts]
    balance = per_member * jnp.sum(load * is_mine) / tok_total
    grad = BALANCE * balance * dense_sum.reshape(-1)[:width] + routed_sum[0]
    router_grad = lax.dynamic_slice(grad, (d * part,), (part,)) * tok_total ** (-0.5)
    return (routed_out, token_grad, router_grad[:, None])


def solution(mesh):
    in_specs = (
        P(("dp", "expert"), None),
        P(None, ("dp", "expert")),
        P(("dp", "expert"), None),
        P("dp", None),
        P("expert", "dp", None, None),
        P("expert", "dp", None),
        P(None, ("dp", "expert"), None),
    )
    out_specs = (P(None, ("dp", "expert"), None), P(("dp", "expert"), None), P("dp", "expert"))
    sizes = (mesh.shape["dp"], mesh.shape["expert"])
    return jax.shard_map(
        functools.partial(on_device, *sizes),
        mesh=mesh,
        in_specs=in_specs,
        out_specs=out_specs,
        check_vma=False,
    )
```

```python
import functools

import jax
import jax.numpy as jnp
import numpy as np
from jax import lax
from jax.experimental import pallas as pl
from jax.experimental.pallas import tpu as pltpu
from jax.sharding import PartitionSpec as P

ROUTE_SCALE = 2.5
BALANCE = 1.0
CAP = 2
STRIDE = 37
MESH = pl.DeviceIdType.MESH
BF16 = jnp.bfloat16
F32 = jnp.float32


def remote(src, dst, send_sem, recv_sem, device):
    return pltpu.make_async_remote_copy(
        src_ref=src,
        dst_ref=dst,
        send_sem=send_sem,
        recv_sem=recv_sem,
        device_id=device,
        device_id_type=MESH,
    )


def take_all(ref, count, sem):
    block = ref.at[pl.ds(0, count)]
    pltpu.make_async_copy(block, block, sem).wait()


def send_rows(n_exp, d, e, source, target, sems):
    def to_peer(s, carry):
        peer = (e + (s * STRIDE) % n_exp) % n_exp
        remote(source.at[peer], target.at[e], sems.at[0], sems.at[1], (d, peer)).start()
        return carry

    lax.fori_loop(1, n_exp, to_peer, 0)


def arrange(group):
    i = np.arange(group * 16)
    quarter, kind, expert, slot = i // (4 * group), i // (2 * group) % 2, i // 2 % group, i % 2
    move = np.zeros((group * 16, group * 16), np.float32)
    move[i, expert * 16 + quarter * 4 + kind * 2 + slot] = 1.0
    return move


def arrange_terms(group):
    i = np.arange(group * 16)
    move = np.zeros((group * 16, group * 16), np.float32)
    move[i, i % 16 * group + i // 16] = 1.0
    return move


def pack(first, second, unmove, quarter):
    parts = []
    for q in range(4):
        columns = slice(q * quarter, (q + 1) * quarter)
        parts += [first[:, columns], second[:, columns]]
    stacked = jnp.concatenate(parts, axis=0)
    return jnp.dot(unmove, stacked, preferred_element_type=F32).astype(BF16)


def layer_kernel(
    n_dp,
    n_exp,
    per_token,
    scale,
    first_ref,
    second_ref,
    tokens_ref,
    cotangent_ref,
    move_ref,
    unmove_ref,
    unterm_ref,
    counts_ref,
    router_ref,
    gate_ref,
    up_ref,
    down_ref,
    routed_ref,
    token_ref,
    router_grad_ref,
    token_hits,
    copy_hits,
    tok,
    cot,
    grad,
    value,
    total_out,
    total_grad,
    rows,
    rows_in,
    terms,
    terms_in,
    router_all,
    slope_s,
    gate_all,
    up_all,
    down_all,
    back,
    land,
    flat,
    dense_s,
    dense_land,
    lifted,
    lifted_land,
    row_sems,
    term_sems,
    self_sems,
    half_sems,
    swap_sems,
    own_send,
    own_recv,
    pass_send,
    pass_recv,
    back_sems,
    back_self,
    dense_sems,
    lifted_sems,
):
    d = lax.axis_index("dp")
    e = lax.axis_index("expert")
    core = e % 2
    sibling = e + 1 - 2 * core
    sides = ((d + 1) % n_dp, (d + n_dp - 1) % n_dp)
    span = gate_ref.shape[0] // 2
    held = (gate_ref, up_ref, down_ref)
    full = (gate_all, up_all, down_all)

    def piece(refs, shard, chunk):
        ref, part = refs[chunk // 2], pl.ds(chunk % 2 * span, span)
        return ref.at[part] if shard is None else ref.at[shard, part]

    orders = ((0, 1, 2, 3, 4, 5), (3, 4, 5, 0, 1, 2))

    def own(side, chunk):
        return remote(
            piece(held, None, chunk),
            piece(full, d, chunk),
            own_send.at[side, chunk],
            own_recv.at[side, chunk],
            (sides[side], e),
        )

    def passed(side, chunk):
        source = sides[1 - side]
        return remote(
            piece(full, source, chunk),
            piece(full, source, chunk),
            pass_send.at[side, chunk % 3],
            pass_recv.at[side, chunk % 3],
            (sides[side], e),
        )

    def router_half(step):
        return remote(
            router_ref.at[core],
            router_all.at[d, core],
            half_sems.at[0, step],
            half_sems.at[1, step],
            ((d + step) % n_dp, e),
        )

    def router_swap(step):
        shard = (d + n_dp - step) % n_dp
        return remote(
            router_all.at[shard, core],
            router_all.at[shard, core],
            swap_sems.at[0, step],
            swap_sems.at[1, step],
            (d, sibling),
        )

    for step in range(1, n_dp):
        router_half(step).start()
    for step in range(6):
        for side in range(2):
            own(side, orders[side][step]).start()
    own_router = pltpu.make_async_copy(router_ref, router_all.at[d], self_sems.at[5])
    own_router.start()
    locals_ = [
        pltpu.make_async_copy(gate_ref, gate_all.at[d], self_sems.at[0]),
        pltpu.make_async_copy(up_ref, up_all.at[d], self_sems.at[1]),
        pltpu.make_async_copy(down_ref, down_all.at[d], self_sems.at[2]),
    ]
    for copy in locals_:
        copy.start()

    first = first_ref[...]
    row_ids = lax.broadcasted_iota(jnp.int32, token_hits.shape, 0)
    hits = row_ids == first[0:1]
    for m in range(1, first.shape[0]):
        hits = hits | (row_ids == first[m : m + 1])
    token_hits[...] = hits.astype(F32).astype(BF16)
    row_ids = lax.broadcasted_iota(jnp.int32, copy_hits.shape, 0)
    copy_hits[...] = (row_ids == second_ref[...]).astype(F32).astype(BF16)
    is_mine = (lax.broadcasted_iota(jnp.int32, (8, n_exp), 1) == e).astype(F32)

    group = unmove_ref.shape[0] // 16
    quarter = rows.shape[2]
    for b in range(n_exp // group):
        at = pl.ds(b * 4 * group, 4 * group)
        placed = jnp.dot(token_hits[at, :], tokens_ref[...], preferred_element_type=F32)
        placed += jnp.dot(copy_hits[at, :], cotangent_ref[...], preferred_element_type=F32)
        placed = placed.astype(BF16)
        rows[pl.ds(b * group, group)] = pack(
            placed[: 2 * group], placed[2 * group :], unmove_ref[...], quarter
        ).reshape(group, 16, quarter)
    send_rows(n_exp, d, e, rows, rows_in, row_sems)
    locals_.append(pltpu.make_async_copy(rows.at[e], rows_in.at[e], self_sems.at[3]))
    locals_[-1].start()

    for step in range(1, n_dp):
        router_half(step).wait_recv()
        router_swap(step).start()
    own_router.wait()
    for step in range(1, n_dp):
        router_swap(step).wait_recv()
    router = router_all[...].reshape(tokens_ref.shape[1], n_exp)
    tokens = tokens_ref[...]
    affinity = jax.nn.sigmoid(jnp.dot(tokens, router, preferred_element_type=F32))
    slope = affinity * (1.0 - affinity)
    slope_s[...] = slope
    dense = lax.dot_general(
        slope.astype(BF16), tokens, (((0,), (0,)), ((), ())), preferred_element_type=F32
    ).astype(BF16)
    lanes = terms.shape[2]
    parts = tokens.shape[1] // lanes
    held_counts = jnp.concatenate(
        [
            jnp.broadcast_to(counts_ref[...].astype(F32), (group, n_exp)),
            jnp.zeros((group, lanes - n_exp), F32),
        ],
        axis=1,
    ).astype(BF16)
    blank = jnp.zeros(((15 - parts) * group, lanes), BF16)
    for b in range(n_exp // group):
        block = [
            dense[b * group : (b + 1) * group, r * lanes : (r + 1) * lanes] for r in range(parts)
        ]
        stack = jnp.concatenate([*block, held_counts, blank], axis=0)
        moved = jnp.dot(unterm_ref[...], stack, preferred_element_type=F32).astype(BF16)
        terms[pl.ds(b * group, group)] = moved.reshape(group, 16, lanes)
    send_rows(n_exp, d, e, terms, terms_in, term_sems)
    locals_.append(pltpu.make_async_copy(terms.at[e], terms_in.at[e], self_sems.at[4]))
    locals_[-1].start()

    for step in range(3):
        for side in range(2):
            chunk = orders[side][step]
            own(side, chunk).wait_recv()
            passed(side, chunk).start()

    transposed = (((1,), (1,)), ((), ()))
    block, part, two = 16 * group, 4 * group, 2 * group
    blocks = n_exp // group
    for copy in locals_:
        copy.wait()
    take_all(rows_in, n_exp - 1, row_sems.at[1])
    for b in range(blocks):
        moved = jnp.dot(
            move_ref[...],
            rows_in[pl.ds(b * group, group)].reshape(block, quarter),
            preferred_element_type=F32,
        ).astype(BF16)
        for q in range(4):
            at = (pl.ds(b * two, two), pl.ds(q * quarter, quarter))
            tok[at] = moved[2 * q * two : (2 * q + 1) * two]
            cot[at] = moved[(2 * q + 1) * two : (2 * q + 2) * two]
    logits = jnp.dot(tok[...], router, preferred_element_type=F32)
    gate = jax.nn.sigmoid(jnp.sum(logits * is_mine[0:1, :], axis=1, keepdims=True))
    value[...] = jnp.broadcast_to(gate, value.shape)
    grad[...] = (ROUTE_SCALE * gate * cot[...].astype(F32)).astype(BF16)

    def expert_part(shard, first):
        gate_w, up_w, down_w = gate_all.at[shard], up_all.at[shard], down_all.at[shard]
        gate_pre = lax.dot_general(tok[...], gate_w[...], transposed, preferred_element_type=F32)
        up_pre = lax.dot_general(tok[...], up_w[...], transposed, preferred_element_type=F32)
        hidden_grad = lax.dot_general(
            grad[...], down_w[...], transposed, preferred_element_type=F32
        )
        squash = jax.nn.sigmoid(gate_pre)
        active = gate_pre * squash
        hidden = (active * up_pre).astype(BF16)
        gate_grad = (hidden_grad * up_pre * squash * (1.0 + gate_pre * (1.0 - squash))).astype(BF16)
        up_grad = (hidden_grad * active).astype(BF16)
        more_out = jnp.dot(hidden, down_w[...], preferred_element_type=F32)
        more_grad = jnp.dot(gate_grad, gate_w[...], preferred_element_type=F32) + jnp.dot(
            up_grad, up_w[...], preferred_element_type=F32
        )
        if first:
            total_out[...] = more_out
            total_grad[...] = more_grad
        else:
            total_out[...] += more_out
            total_grad[...] += more_grad

    expert_part(d, True)
    for side in range(2):
        for step in range(3, 6):
            own(side, orders[side][step]).wait_recv()
        expert_part(sides[1 - side], False)
    take_all(terms_in, n_exp - 1, term_sems.at[1])
    dense_s[...] = jnp.sum(terms_in[...].astype(F32), axis=0)
    for step in range(3):
        for side in range(2):
            passed(side, orders[side][step]).wait_recv()
    expert_part((d + 2) % n_dp, False)

    gate = value[:, 0:1]
    expert_out = total_out[...].astype(BF16).astype(F32)
    affinity_grad = ROUTE_SCALE * jnp.sum(
        cot[...].astype(F32) * expert_out, axis=1, keepdims=True
    )
    lift = gate * (1.0 - gate) * affinity_grad
    column = lax.dot_general(
        is_mine.astype(BF16), router, transposed, preferred_element_type=F32
    )[0:1]
    lifted[...] = jnp.broadcast_to(
        jnp.sum(lift * tok[...].astype(F32), axis=0, keepdims=True), lifted.shape
    )

    def small(shift, ref, target, sems):
        return remote(
            ref,
            target.at[d],
            sems.at[0, shift],
            sems.at[1, shift],
            ((d + shift) % n_dp, e),
        )

    smalls = []
    for shift in range(1, n_dp):
        smalls.append(small(shift, dense_s, dense_land, dense_sems))
        smalls.append(small(shift, lifted, lifted_land, lifted_sems))
    for copy in smalls:
        copy.start()
    grad[...] = (total_grad[...] + lift * column).astype(BF16)
    tok[...] = (ROUTE_SCALE * gate * expert_out).astype(BF16)
    for b in range(blocks):
        at = pl.ds(b * two, two)
        back[pl.ds(b * group, group)] = pack(
            grad[at, :], tok[at, :], unmove_ref[...], quarter
        ).reshape(group, 16, quarter)
    send_rows(n_exp, d, e, back, land, back_sems)
    returns = (
        pltpu.make_async_copy(back.at[e], land.at[e], back_self.at[0]),
        pltpu.make_async_copy(dense_s, dense_land.at[d], back_self.at[1]),
        pltpu.make_async_copy(lifted, lifted_land.at[d], back_self.at[2]),
    )
    for copy in returns:
        copy.start()
    for copy in returns:
        copy.wait()
    for copy in smalls:
        copy.wait()
    all_dense = jnp.sum(dense_land[...], axis=0)
    all_lifted = jnp.sum(lifted_land[...], axis=0)[0:1]
    pieces = tok.shape[1] // all_dense.shape[1]
    load = all_dense[pieces : pieces + 1, :n_exp]
    my_load = jnp.sum(load * is_mine[0:1], axis=1, keepdims=True)
    dense_row = jnp.concatenate([all_dense[r : r + 1] for r in range(pieces)], axis=1)
    router_terms = (BALANCE * (per_token * my_load) * dense_row + all_lifted) * scale
    share = router_grad_ref.shape[1]
    for p in range(n_dp):

        @pl.when(d == p)
        def _(p=p):
            router_grad_ref[...] = router_terms[:, p * share : (p + 1) * share]

    spread = (slope_s[...] * (BALANCE * (per_token * load))).astype(BF16)
    router_back = lax.dot_general(
        spread, router, transposed, preferred_element_type=F32
    )

    take_all(back, n_exp - 1, back_sems.at[0])
    take_all(land, n_exp - 1, back_sems.at[1])
    for b in range(blocks):
        moved = jnp.dot(
            move_ref[...],
            land[pl.ds(b * group, group)].reshape(block, quarter),
            preferred_element_type=F32,
        ).astype(BF16)
        for q in range(4):
            flat[pl.ds(b * part, part), pl.ds(q * quarter, quarter)] = moved[
                q * part : (q + 1) * part
            ]
    over_rows = (((0,), (0,)), ((), ()))
    home = lax.dot_general(token_hits[...], flat[...], over_rows, preferred_element_type=F32)
    token_ref[...] = (home + router_back).astype(BF16)
    routed_ref[...] = lax.dot_general(
        copy_hits[...], flat[...], over_rows, preferred_element_type=F32
    ).astype(BF16)

    for step in range(1, n_dp):
        router_half(step).wait_send()
        router_swap(step).wait_send()
    for step in range(6):
        for side in range(2):
            own(side, orders[side][step]).wait_send()
    for step in range(3):
        for side in range(2):
            passed(side, orders[side][step]).wait_send()
    take_all(rows, n_exp - 1, row_sems.at[0])
    take_all(terms, n_exp - 1, term_sems.at[0])


def layer(n_dp, n_exp, per_token, scale, wholes, weights):
    own, cotangent = wholes[2:4]
    tokens, width = own.shape
    slots = n_exp * CAP
    hidden = weights[0].shape[0]

    def out(*shape, kind=BF16):
        return jax.ShapeDtypeStruct(shape, kind)

    def vmem(*shape, kind=BF16):
        return pltpu.VMEM(shape, kind)

    message = vmem(n_exp, 16, width // 4)
    terms = vmem(n_exp, 16, 256)
    gathered = vmem(n_dp, hidden, width)
    dma = pltpu.SemaphoreType.DMA
    return pl.pallas_call(
        functools.partial(layer_kernel, n_dp, n_exp, per_token, scale),
        name="layer",
        out_shape=(
            out(*cotangent.shape),
            out(tokens, width),
            out(1, width // n_dp, kind=F32),
        ),
        in_specs=[pl.BlockSpec(memory_space=pltpu.VMEM)] * 9
        + [pl.BlockSpec(memory_space=pl.ANY)] * 3,
        out_specs=[pl.BlockSpec(memory_space=pltpu.VMEM)] * 3,
        scratch_shapes=[
            vmem(2 * slots, tokens),
            vmem(2 * slots, cotangent.shape[0]),
            *[vmem(slots, width)] * 3,
            vmem(slots, 128, kind=F32),
            *[vmem(slots, width, kind=F32)] * 2,
            *[message] * 2,
            *[terms] * 2,
            vmem(n_dp, *wholes[8].shape),
            vmem(tokens, n_exp, kind=F32),
            *[gathered] * 3,
            *[message] * 2,
            vmem(2 * slots, width),
            vmem(16, 256, kind=F32),
            vmem(n_dp, 16, 256, kind=F32),
            vmem(8, width, kind=F32),
            vmem(n_dp, 8, width, kind=F32),
            dma((2,)),
            dma((2,)),
            dma((6,)),
            dma((2, n_dp)),
            dma((2, n_dp)),
            dma((2, 6)),
            dma((2, 6)),
            dma((2, 3)),
            dma((2, 3)),
            dma((2,)),
            dma((3,)),
            dma((2, n_dp)),
            dma((2, n_dp)),
        ],
        compiler_params=pltpu.CompilerParams(
            has_side_effects=True, vmem_limit_bytes=60 << 20
        ),
    )(*wholes, *weights)


def on_device(n_dp, n_exp, tokens, routes, counts, router, gate_up_weight, down_weight, cotangent):
    members, tok_local = routes.shape
    width = tokens.shape[1]
    experts = router.shape[1]
    per_member = experts // members
    copies = members * tok_local
    tok_total = tok_local * n_dp * n_exp
    part = width // n_dp

    earlier = (
        (routes[:, :, None] == routes[:, None, :])
        & (jnp.arange(tok_local)[None, None, :] < jnp.arange(tok_local)[None, :, None])
    ).astype(jnp.int32)
    rank = jnp.sum(earlier, axis=2)
    owners = routes + per_member * jnp.arange(members, dtype=jnp.int32)[:, None]
    group = min(16, experts)
    move_np = arrange(group)
    move, unmove = jnp.asarray(move_np, BF16), jnp.asarray(move_np.T, BF16)
    first = owners // group * (4 * group) + owners % group * CAP + rank
    second = first + 2 * group
    wholes = (
        first,
        second.reshape(1, copies),
        tokens,
        cotangent.reshape(copies, width),
        move,
        unmove,
        jnp.asarray(arrange_terms(group), BF16),
        counts,
        router.reshape(2, part // 2, experts),
    )
    weights = (gate_up_weight[0, :, 0, :], gate_up_weight[0, :, 1, :], down_weight[0])
    routed_out, token_grad, router_grad = layer(
        n_dp, n_exp, per_member / tok_total, tok_total ** (-0.5), wholes, weights
    )
    routed_out = routed_out.reshape(members, tok_local, width)
    return (routed_out, token_grad, router_grad.reshape(part, 1))


def solution(mesh):
    in_specs = (
        P(("dp", "expert"), None),
        P(None, ("dp", "expert")),
        P(("dp", "expert"), None),
        P("dp", None),
        P("expert", "dp", None, None),
        P("expert", "dp", None),
        P(None, ("dp", "expert"), None),
    )
    out_specs = (P(None, ("dp", "expert"), None), P(("dp", "expert"), None), P("dp", "expert"))
    sizes = (mesh.shape["dp"], mesh.shape["expert"])
    return jax.shard_map(
        functools.partial(on_device, *sizes),
        mesh=mesh,
        in_specs=in_specs,
        out_specs=out_specs,
        check_vma=False,
    )
```
